128 devices in a mesh: wave: 8 (over y, core), fly: 16 (over x, z).
Axes of the slice: x: 4, y: 4, z: 4, core: 2. Of those that a mesh axis runs over, the one named last changes fastest.
Arguments:
- grid_fourier: bfloat16 [2048, 256, 768], P(('fly', 'wave')), may hold values from -6 to 6
- m_slot: int32 [256], replicated, may hold values from 0 to 255, each once
- compress: bfloat16 [2048, 256, 64], P('fly', 'wave'), may hold values from -0.5 to 0.5
- mix: float32 [16, 256, 256, 128], P('fly', 'wave'), may hold values from -0.5 to 0.5
- expand: float32 [2048, 256, 64], P('fly', 'wave'), may hold values from -0.75 to 0.75
Outputs:
- spectral: float32 [2048, 256, 768], P('fly', 'wave')
The draws below stay inside these ranges and needn't reach their ends.
Inputs may be any that keep to these rules, and one draw needn't show every extreme that they name: `m_slot`: each wavenumber 0 .. 255 stands in exactly one slot.
All inputs are finite; a program needn't handle non-finite values.
Results may differ from the reference program's by a relative error of at most 0.0003.
Values may be sent and summed in bfloat16 or wider, within the bound.
A program may use at most 128 MiB of HBM per device.

```python
import jax
import jax.numpy as jnp
from jax import lax

RANK = 64
LAT_DEV = 128
COLS = 768
LEVELS = 4
LAT = 2048
NDEG = 2048
M_WIN = 256
N_FLY = 16


def shard_levels(stream_key, shape, split, least, largest):
    def one(position, blocks):
        heights = jax.random.uniform(jax.random.fold_in(jax.random.fold_in(stream_key, 6), position), (blocks,), jnp.float32, least / len(split), largest / len(split))
        return jnp.repeat(jnp.exp(heights), shape[position] // blocks).reshape((-1,) + (1,) * (len(shape) - position - 1))

    gain = one(*split[0])
    for cut in split[1:]:
        gain = gain * one(*cut)
    return gain


def noise(key, shape, scale, most, split=(), held_as=jnp.bfloat16):
    array = jax.random.normal(key, shape, jnp.float32) * scale
    if len(split) > 0:
        array = shard_levels(key, shape, split, -0.22, 0.18) * array
    return jnp.clip(array, min=-most, max=most).astype(held_as)


def setup_inputs(seed: int = 0) -> dict:
    arg_keys = jax.random.split(jax.random.key(seed), 6)
    return {
        "grid_fourier": noise(arg_keys[0], (LAT, M_WIN, COLS), 1.0, 6.0, ((0, 128),)),
        "m_slot": jax.random.permutation(arg_keys[1], M_WIN).astype(jnp.int32),
        "compress": noise(arg_keys[2], (LAT, M_WIN, RANK), LAT_DEV ** -0.5, 0.5, ((0, 16), (1, 8))),
        "mix": noise(arg_keys[3], (N_FLY, M_WIN, LEVELS * RANK, 2 * RANK), (2 * RANK) ** -0.5, 0.5, ((0, 16), (1, 8)), jnp.float32),
        "expand": noise(arg_keys[4], (NDEG, M_WIN, RANK), RANK ** -0.5, 0.75, ((0, 16), (1, 8)), jnp.float32),
    }


highest = lax.Precision.HIGHEST


def one_slot(slot, grid_fourier, m_slot, compress, mix, expand):
    wave_number = m_slot[slot]
    column = lax.dynamic_index_in_dim(grid_fourier, wave_number, 1, keepdims=False).astype(jnp.float32)
    slot_compress = compress[:, slot, :].astype(jnp.float32)
    slot_mix = mix[:, slot]
    slot_expand = expand[:, slot, :]
    carried = jnp.einsum("flc,flk->fkc", column.reshape(N_FLY, LAT_DEV, COLS), slot_compress.reshape(N_FLY, LAT_DEV, RANK), precision=highest)
    places = jnp.arange(N_FLY, dtype=jnp.int32)
    for bit_level in range(LEVELS):
        partner = carried[jnp.bitwise_xor(places, 1 << bit_level)]
        own_low = (jnp.right_shift(places, bit_level) & 1) == 0
        lower_part = jnp.where(own_low[:, None, None], carried, partner)
        upper_part = jnp.where(own_low[:, None, None], partner, carried)
        factor = slot_mix[:, bit_level * RANK:(bit_level + 1) * RANK, :]
        carried = jnp.einsum("fkj,fjc->fkc", factor[..., :RANK], lower_part, precision=highest) + jnp.einsum("fkj,fjc->fkc", factor[..., RANK:], upper_part, precision=highest)
    coeffs = jnp.einsum("fdk,fkc->fdc", slot_expand.reshape(N_FLY, LAT_DEV, RANK), carried, precision=highest).reshape(NDEG, COLS)
    exists = jnp.arange(NDEG, dtype=jnp.int32) >= wave_number
    return jnp.where(exists[:, None], coeffs, jnp.zeros_like(coeffs))


def reference(grid_fourier, m_slot, compress, mix, expand):
    stacked = lax.map(lambda slot: one_slot(slot, grid_fourier, m_slot, compress, mix, expand), jnp.arange(M_WIN, dtype=jnp.int32))
    return jnp.transpose(stacked, (1, 0, 2))
```

```python
import functools

import jax
import jax.numpy as jnp
from jax import lax
from jax.experimental import pallas as pl
from jax.experimental.pallas import tpu as pltpu
from jax.sharding import PartitionSpec as P

MESH = pl.DeviceIdType.MESH
F32, BF16, I16, I32 = jnp.float32, jnp.bfloat16, jnp.int16, jnp.int32

CB = 384
GROUP = 4
LEAD = 3
QMAX = 32766.0


def quantize(x):
    largest = jnp.maximum(jnp.max(jnp.abs(x), axis=0, keepdims=True), 1e-30)
    q = jnp.round(x * (QMAX / largest)).astype(I32).astype(I16)
    return q, largest * (1.0 / QMAX)


def restore(q, scale):
    return q.astype(I32).astype(F32) * scale


def split(x):
    high = x.astype(BF16)
    return high, (x - high.astype(F32)).astype(BF16)


def product(a, b):
    (ah, al), (bh, bl) = split(a), split(b)
    dot = functools.partial(jnp.dot, preferred_element_type=F32)
    return dot(ah, bh) + (dot(ah, bl) + dot(al, bh))


def exchange_kernel(
    m_slot, comp_hbm, grid, mix, out_q, out_s,
    gbuf, tr, ysend, yrecv, mixf,
    mzs, mzss, mzr, mzrs, mxs, mxss, mxr, mxrs,
    z1s, z1ss, z1r, z1rs, z2s, z2ss, z2r, z2rs, x1r, x1rs, x2s, x2ss,
    onehot, comp, load_sem, comp_sem, mix_sem, send_sem, y_sem, m_sem, z1_sem, z2_sem, x1_sem, o_sem,
):
    units, waves = ysend.shape[0], ysend.shape[1]
    lats = ysend.shape[3]
    n_cb = gbuf.shape[0]
    chunks = units // n_cb
    w, f = lax.axis_index("wave"), lax.axis_index("fly")
    my_x, my_z = f // GROUP, lax.rem(f, GROUP)

    def z_dev(j):
        return (w, my_x * GROUP + j)

    def x_dev(j):
        return (w, j * GROUP + my_z)

    def other(mine, d):
        return lax.rem(mine + d, GROUP)

    for cb in range(n_cb):
        pltpu.make_async_copy(
            grid.at[:, :, pl.ds(cb * CB, CB)], gbuf.at[cb], load_sem.at[cb]
        ).start()
    pltpu.make_async_copy(comp_hbm, comp, comp_sem).start()
    pltpu.make_async_copy(mix, mixf, mix_sem).start()

    wave_number = lax.broadcasted_iota(I32, onehot.shape, 0)
    onehot[...] = jnp.transpose((wave_number == m_slot[...]).astype(F32)).astype(BF16)

    barrier = pltpu.get_barrier_semaphore()
    peers = [(lax.rem(w + d, waves), f) for d in range(1, waves)]
    for d in range(1, GROUP):
        peers += [z_dev(other(my_z, d)), x_dev(other(my_x, d))]
    for peer in peers:
        pl.semaphore_signal(barrier, inc=1, device_id=peer, device_id_type=MESH)
    pl.semaphore_wait(barrier, len(peers))

    def push(src, dst, send, recv, peer):
        pltpu.make_async_remote_copy(
            src_ref=src, dst_ref=dst, send_sem=send, recv_sem=recv,
            device_id=peer, device_id_type=MESH,
        ).start()

    def arrive(ref, sem):
        pltpu.make_async_copy(ref, ref, sem).wait()

    def transpose(cb):
        arrive(gbuf.at[cb], load_sem.at[cb])

        def one(l, _):
            x = jnp.dot(onehot[...], gbuf[cb, l], preferred_element_type=F32)
            for c in range(CB // 128):
                rows = pl.ds(l, gbuf.shape[2], stride=lats)
                tr[c, rows, :] = x[:, c * 128 : (c + 1) * 128]
            return 0

        lax.fori_loop(0, lats, one, 0)

    def stage_gather(u):
        cb, ch = u // chunks, lax.rem(u, chunks)
        pl.when(ch == 0)(lambda: transpose(cb))
        for d in range(waves):
            to = lax.rem(w + d, waves)
            for j in range(GROUP):
                slot = (to * chunks + ch) * GROUP + j
                rows = pl.ds(pl.multiple_of(slot * lats, lats), lats)
                for c in range(CB // 128):
                    ysend[u, to, j, :, pl.ds(c * 128, 128)] = tr[c, rows, :].astype(BF16)
            dst = yrecv.at[u, :, pl.ds(pl.multiple_of(w * lats, lats), lats), :]
            if d == 0:
                pltpu.make_async_copy(ysend.at[u, to], dst, y_sem.at[u]).start()
            else:
                push(ysend.at[u, to], dst, send_sem.at[0], y_sem.at[u], (to, f))

    def prepare_mix():
        arrive(mixf, mix_sem)

        def one(ch, _):
            for j in range(GROUP):
                for level in range(4):
                    q, s = quantize(mixf[ch * GROUP + j, level * 64 : (level + 1) * 64, :])
                    sq, ss = ((mzs, mzss), (mxs, mxss))[level // 2]
                    sq[j, ch, (level % 2) * 64 : (level % 2 + 1) * 64, :] = q
                    ss[j, ch, level % 2] = s
            return 0

        lax.fori_loop(0, chunks, one, 0)
        for mine, dev, sq, ss, rq, rs, k in (
            (my_z, z_dev, mzs, mzss, mzr, mzrs, 0),
            (my_x, x_dev, mxs, mxss, mxr, mxrs, 1),
        ):
            for d in range(1, GROUP):
                j = other(mine, d)
                push(sq.at[j], rq.at[mine], send_sem.at[1 + k], m_sem.at[2 * k], dev(j))
                push(ss.at[j], rs.at[mine], send_sem.at[3 + k], m_sem.at[2 * k + 1], dev(j))
            pltpu.make_async_copy(sq.at[mine], rq.at[mine], m_sem.at[2 * k]).start()
            pltpu.make_async_copy(ss.at[mine], rs.at[mine], m_sem.at[2 * k + 1]).start()

    def spread(u, d, mine, dev, sq, ss, dq, ds, k, sem):
        j = other(mine, d)
        if d == 0:
            pltpu.make_async_copy(sq.at[u, j], dq.at[u, mine], sem.at[0, u]).start()
            pltpu.make_async_copy(ss.at[u, j], ds.at[u, mine], sem.at[1, u]).start()
        else:
            push(sq.at[u, j], dq.at[u, mine], send_sem.at[k], sem.at[0, u], dev(j))
            push(ss.at[u, j], ds.at[u, mine], send_sem.at[k + 1], sem.at[1, u], dev(j))

    def stage_compress(u):
        ch = lax.rem(u, chunks)
        pl.when(u == 0)(lambda: arrive(comp, comp_sem))
        arrive(yrecv.at[u], y_sem.at[u])
        for d in (2, 1, 3, 0):
            j = other(my_z, d)
            acc = jnp.dot(comp[ch * GROUP + j], yrecv[u, j], preferred_element_type=F32)
            z1s[u, j], z1ss[u, j] = quantize(acc)
            spread(u, d, my_z, z_dev, z1s, z1ss, z1r, z1rs, 5, z1_sem)

    def two_levels(u, ch, rq, rs, mq, ms, sq, ss):
        blocks = [restore(rq[u, b], rs[u, b]) for b in range(GROUP)]
        for level in range(2):
            new = list(blocks)
            for lower in range(GROUP):
                if lower >> level & 1:
                    continue
                upper = lower | 1 << level
                factor = jnp.concatenate(
                    [
                        restore(mq[b, ch, level * 64 : (level + 1) * 64, :], ms[b, ch, level])
                        for b in (lower, upper)
                    ],
                    axis=0,
                )
                out = product(factor, jnp.concatenate([blocks[lower], blocks[upper]], axis=0))
                new[lower], new[upper] = out[:64], out[64:]
            blocks = new
        for b in range(GROUP):
            sq[u, b], ss[u, b] = quantize(blocks[b])

    def stage_low(u):
        ch = lax.rem(u, chunks)

        @pl.when(u == 0)
        def _():
            arrive(mzr, m_sem.at[0])
            arrive(mzrs, m_sem.at[1])

        arrive(z1r.at[u], z1_sem.at[0, u])
        arrive(z1rs.at[u], z1_sem.at[1, u])
        two_levels(u, ch, z1r, z1rs, mzr, mzrs, z2s, z2ss)
        for d in (2, 1, 3, 0):
            spread(u, d, my_z, z_dev, z2s, z2ss, z2r, z2rs, 7, z2_sem)

    def stage_turn(u):
        arrive(z2r.at[u], z2_sem.at[0, u])
        arrive(z2rs.at[u], z2_sem.at[1, u])
        for d in (2, 1, 3, 0):
            spread(u, d, my_x, x_dev, z2r, z2rs, x1r, x1rs, 9, x1_sem)

    def stage_high(u):
        ch = lax.rem(u, chunks)

        @pl.when(u == 0)
        def _():
            arrive(mxr, m_sem.at[2])
            arrive(mxrs, m_sem.at[3])

        arrive(x1r.at[u], x1_sem.at[0, u])
        arrive(x1rs.at[u], x1_sem.at[1, u])
        two_levels(u, ch, x1r, x1rs, mxr, mxrs, x2s, x2ss)
        for d in (2, 1, 3, 0):
            j = other(my_x, d)
            if d == 0:
                pltpu.make_async_copy(x2s.at[u, j], out_q.at[u, my_x], o_sem.at[0]).start()
                pltpu.make_async_copy(x2ss.at[u, j], out_s.at[u, my_x], o_sem.at[1]).start()
            else:
                push(x2s.at[u, j], out_q.at[u, my_x], send_sem.at[11], o_sem.at[0], x_dev(j))
                push(x2ss.at[u, j], out_s.at[u, my_x], send_sem.at[12], o_sem.at[1], x_dev(j))

    def step(t, _):
        for lag, stage in (
            (LEAD + 6, stage_high),
            (LEAD + 4, stage_turn),
            (LEAD + 2, stage_low),
            (LEAD, stage_compress),
            (0, stage_gather),
        ):
            u = t - lag
            pl.when((u >= 0) & (u < units))(functools.partial(stage, u))
        pl.when(t == LEAD - 1)(prepare_mix)
        return 0

    lax.fori_loop(0, units + LEAD + 6, step, 0)

    arrive(out_q, o_sem.at[0])
    arrive(out_s, o_sem.at[1])
    arrive(ysend.at[:, pl.ds(0, waves - 1)], send_sem.at[0])
    sent = pl.ds(0, GROUP - 1)
    for k, ref in enumerate((mzs, mxs, mzss, mxss)):
        arrive(ref.at[sent], send_sem.at[1 + k])
    for k, ref in enumerate((z1s, z1ss, z2s, z2ss, z2r, z2rs, x2s, x2ss)):
        arrive(ref.at[:, sent], send_sem.at[5 + k])


def exchange(m_slot, comp, grid, mix, waves):
    lats, all_slots, cols = grid.shape
    slots, rank, width = comp.shape
    n_cb = cols // CB
    chunks = slots // GROUP
    units = n_cb * chunks
    parts = (units, GROUP, rank, CB)
    scales = (units, GROUP, 1, CB)
    mq = (GROUP, chunks, 2 * rank, 2 * rank)
    ms = (GROUP, chunks, 2, 1, 2 * rank)
    vmem = pltpu.VMEM
    any_spec = pl.BlockSpec(memory_space=pl.ANY)
    return pl.pallas_call(
        exchange_kernel,
        out_shape=(jax.ShapeDtypeStruct(parts, I16), jax.ShapeDtypeStruct(scales, F32)),
        in_specs=[
            pl.BlockSpec(memory_space=pltpu.VMEM),
            any_spec,
            any_spec,
            any_spec,
        ],
        out_specs=(any_spec, any_spec),
        scratch_shapes=[
            vmem((n_cb, lats, all_slots, CB), BF16),
            vmem((CB // 128, all_slots * lats, 128), F32),
            vmem((units, waves, GROUP, lats, CB), BF16),
            vmem((units, GROUP, width, CB), BF16),
            vmem(mix.shape, F32),
            vmem(mq, I16), vmem(ms, F32), vmem(mq, I16), vmem(ms, F32),
            vmem(mq, I16), vmem(ms, F32), vmem(mq, I16), vmem(ms, F32),
            vmem(parts, I16), vmem(scales, F32), vmem(parts, I16), vmem(scales, F32),
            vmem(parts, I16), vmem(scales, F32), vmem(parts, I16), vmem(scales, F32),
            vmem(parts, I16), vmem(scales, F32),
            vmem(parts, I16), vmem(scales, F32),
            vmem((all_slots, all_slots), BF16),
            vmem(comp.shape, BF16),
            pltpu.SemaphoreType.DMA((n_cb,)),
            pltpu.SemaphoreType.DMA,
            pltpu.SemaphoreType.DMA,
            pltpu.SemaphoreType.DMA((13,)),
            pltpu.SemaphoreType.DMA((units,)),
            pltpu.SemaphoreType.DMA((4,)),
            pltpu.SemaphoreType.DMA((2, units)),
            pltpu.SemaphoreType.DMA((2, units)),
            pltpu.SemaphoreType.DMA((2, units)),
            pltpu.SemaphoreType.DMA((2,)),
        ],
        compiler_params=pltpu.CompilerParams(
            collective_id=0, has_side_effects=True, vmem_limit_bytes=60 * 2**20
        ),
        name="exchange",
    )(m_slot[None, :], comp, grid, mix)


def expand_kernel(m_slot, q_ref, s_ref, e_ref, out_ref):
    slots = e_ref.shape[0]
    degrees = e_ref.shape[2]
    group = pl.program_id(1)
    groups = pl.num_programs(1)
    first = lax.axis_index("fly") * degrees
    base = (lax.axis_index("wave") * groups + group) * slots
    degree = first + lax.broadcasted_iota(I32, (degrees, CB), 0)
    dot = functools.partial(
        lax.dot_general,
        dimension_numbers=(((0,), (0,)), ((), ())),
        preferred_element_type=F32,
    )
    for i in range(slots):
        eh, el = split(e_ref[i])
        qh, ql = split(q_ref[i // GROUP, i % GROUP].astype(I32).astype(F32))
        val = dot(eh, qh) + (dot(eh, ql) + dot(el, qh))
        val = val * s_ref[i // GROUP, i % GROUP]
        out_ref[:, i, :] = jnp.where(degree >= m_slot[base + i], val, 0.0)


def expand_out(m_slot, q, s, exp_t):
    units, _, rank, _ = q.shape
    slots, _, degrees = exp_t.shape
    n_cb = units * GROUP // slots
    per = 8 // GROUP
    groups = slots // 8
    return pl.pallas_call(
        expand_kernel,
        grid=(n_cb, groups),
        out_shape=jax.ShapeDtypeStruct((degrees, slots, n_cb * CB), F32),
        in_specs=[
            pl.BlockSpec(memory_space=pltpu.SMEM),
            pl.BlockSpec((per, GROUP, rank, CB), lambda c, g: (c * groups + g, 0, 0, 0)),
            pl.BlockSpec((per, GROUP, 1, CB), lambda c, g: (c * groups + g, 0, 0, 0)),
            pl.BlockSpec((8, rank, degrees), lambda c, g: (g, 0, 0)),
        ],
        out_specs=pl.BlockSpec((degrees, 8, CB), lambda c, g: (0, g, c)),
        compiler_params=pltpu.CompilerParams(vmem_limit_bytes=32 * 2**20),
        name="expand_out",
    )(m_slot, q, s, exp_t)


def on_device(grid_fourier, m_slot, compress, mix, expand):
    comp = jnp.transpose(compress, (1, 2, 0))
    exp_t = jnp.transpose(expand, (1, 2, 0))
    waves = lax.axis_size("wave")
    q, s = exchange(m_slot, comp, grid_fourier, mix[0], waves)
    return expand_out(m_slot, q, s, exp_t)


def solution(mesh):
    in_specs = (
        P(("fly", "wave"), None, None),
        P(),
        P("fly", "wave", None),
        P("fly", "wave", None, None),
        P("fly", "wave", None),
    )
    return jax.shard_map(
        on_device, mesh=mesh, in_specs=in_specs, out_specs=P("fly", "wave", None),
        check_vma=False,
    )
```

```python
import functools

import jax
import jax.numpy as jnp
from jax import lax
from jax.experimental import pallas as pl
from jax.experimental.pallas import tpu as pltpu
from jax.sharding import PartitionSpec as P

MESH = pl.DeviceIdType.MESH
F32, BF16, I16, I32 = jnp.float32, jnp.bfloat16, jnp.int16, jnp.int32

CB = 256
GROUP = 4
LAG = 3
LEAD = 4
QMAX = 32766.0
SPLIT = 2


def quantize(x):
    largest = jnp.maximum(jnp.max(jnp.abs(x), axis=0, keepdims=True), 1e-30)
    q = jnp.round(x * (QMAX / largest)).astype(I32).astype(I16)
    return q, largest * (1.0 / QMAX)


def restore(q, scale):
    return q.astype(I32).astype(F32) * scale


def split(x):
    high = x.astype(BF16)
    return high, (x - high.astype(F32)).astype(BF16)


def product(ah, al, b):
    bh, bl = split(b)
    left = jnp.concatenate([ah, ah, al], axis=1)
    return jnp.dot(left, jnp.concatenate([bh, bl, bh], axis=0), preferred_element_type=F32)


def pairs(level):
    return [(b, b | 1 << level) for b in range(GROUP) if not b >> level & 1]


def exchange_kernel(
    m_slot, comp_hbm, grid, mix, out_q, out_s,
    gbuf, flat, ysend, yrecv,
    mzs, mzss, mzr, mzrs, mxs, mxss, mxr, mxrs, fzh, fzl, fxh, fxl,
    z1s, z1ss, z1r, z1rs, z2s, z2ss, x1r, x1rs, x2s, x2ss,
    onehot, comp, load_sem, comp_sem, mix_sem, send_sem, y_sem, m_sem, z1_sem, x1_sem, o_sem,
):
    units, lats = ysend.shape[0], ysend.shape[2]
    waves = ysend.shape[1] // GROUP
    n_cb = gbuf.shape[0]
    chunks = units // n_cb
    w, f = lax.axis_index("wave"), lax.axis_index("fly")
    my_x, my_z = f // GROUP, lax.rem(f, GROUP)

    def z_dev(j):
        return (w, my_x * GROUP + j)

    def x_dev(j):
        return (w, j * GROUP + my_z)

    def other(mine, d):
        return lax.rem(mine + d, GROUP)

    for cb in range(n_cb):
        pltpu.make_async_copy(
            grid.at[:, :, pl.ds(cb * CB, CB)], gbuf.at[cb], load_sem.at[cb]
        ).start()
    pltpu.make_async_copy(comp_hbm, comp, comp_sem).start()
    halves = [
        (pl.ds(h * lats, lats), flat.at[1, :, :, pl.ds(h * 128, 128)]) for h in range(2)
    ]
    for part, dst in halves:
        pltpu.make_async_copy(mix.at[part], dst, mix_sem).start()

    barrier = pltpu.get_barrier_semaphore()
    peers = [(lax.rem(w + d, waves), f) for d in range(1, waves)]
    peers += [(w, lax.rem(f + d, GROUP * GROUP)) for d in range(1, GROUP * GROUP)]
    for peer in peers:
        pl.semaphore_signal(barrier, inc=1, device_id=peer, device_id_type=MESH)

    sent = pl.ds(0, GROUP - 1)

    def push(src, dst, send, recv, peer):
        pltpu.make_async_remote_copy(
            src_ref=src, dst_ref=dst, send_sem=send, recv_sem=recv,
            device_id=peer, device_id_type=MESH,
        ).start()

    def arrive(ref, sem):
        pltpu.make_async_copy(ref, ref, sem).wait()

    def pick(cb, l):
        flat[lax.rem(cb, 2), l] = jnp.dot(onehot[...], gbuf[cb, l], preferred_element_type=F32)

    def arrange(u):
        cb, ch = u // chunks, lax.rem(u, chunks)
        for r in range(0, waves * GROUP, 8):
            rows = pl.ds(pl.multiple_of(ch * (waves * GROUP) + r, 8), 8)
            for c in range(0, CB, 128):
                x = flat[lax.rem(cb, 2), :, rows, c : c + 128]
                ysend[u, r : r + 8, :, c : c + 128] = pltpu.einshape("lsc->slc", x).astype(BF16)

    def send_wave(u):
        dst = yrecv.at[u, :, pl.ds(pl.multiple_of(w * lats, lats), lats), :]
        for d in range(1, waves):
            to = lax.rem(w + d, waves)
            push(ysend.at[u, pl.ds(to * GROUP, GROUP)], dst, send_sem.at[0], y_sem.at[u], (to, f))
        pltpu.make_async_copy(ysend.at[u, pl.ds(w * GROUP, GROUP)], dst, y_sem.at[u]).start()

    def stage_gather(u):
        arrange(u)
        send_wave(u)
        pick_next(u)

    def pick_next(u):
        cb, ch = u // chunks, lax.rem(u, chunks)
        for k in range(1, n_cb):
            first = (k - 1) * chunks
            pl.when(u == first)(lambda k=k: arrive(gbuf.at[k], load_sem.at[k]))

        @pl.when(cb + 1 < n_cb)
        def _():
            for i in range(lats // chunks):
                pick(cb + 1, ch * (lats // chunks) + i)

    def high_dev(j, b, ch):
        return lax.rem(j + b + 2 * lax.rem(ch, 2), GROUP)

    def high_slot(ch):
        return lax.rem(my_x - my_z - 2 * lax.rem(ch, 2) + 2 * GROUP, GROUP)

    def prepare_mix():
        arrive(flat.at[1], mix_sem)

        def one(ch, _):
            for j in range(GROUP):
                for level in range(4):
                    at = lax.rem(ch * GROUP + j, lats)
                    cols = pl.ds(pl.multiple_of(ch * GROUP // lats * 128, 128), 128)
                    q, s = quantize(flat[1, at, level * 64 : (level + 1) * 64, cols])
                    if level < 2:
                        sq, ss, to = mzs, mzss, j
                    else:
                        sq, ss, to = mxs, mxss, high_dev(j, my_z, ch)
                    sq[to, ch, (level % 2) * 64 : (level % 2 + 1) * 64, :] = q
                    ss[to, ch, level % 2] = s
            return 0

        lax.fori_loop(0, chunks, one, 0)

    def send_mix():
        for mine, dev, sq, ss, rq, rs, k in (
            (my_z, z_dev, mzs, mzss, mzr, mzrs, 0),
            (my_x, x_dev, mxs, mxss, mxr, mxrs, 1),
        ):
            for d in range(1, GROUP):
                j = other(mine, d)
                push(sq.at[j], rq.at[mine], send_sem.at[1 + k], m_sem.at[2 * k], dev(j))
                push(ss.at[j], rs.at[mine], send_sem.at[3 + k], m_sem.at[2 * k + 1], dev(j))
            pltpu.make_async_copy(sq.at[mine], rq.at[mine], m_sem.at[2 * k]).start()
            pltpu.make_async_copy(ss.at[mine], rs.at[mine], m_sem.at[2 * k + 1]).start()

    def copy_pair(sq, ss, dq, ds, k, qsem, ssem, peer):
        if peer is None:
            pltpu.make_async_copy(sq, dq, qsem).start()
            pltpu.make_async_copy(ss, ds, ssem).start()
        else:
            push(sq, dq, send_sem.at[k], qsem, peer)
            push(ss, ds, send_sem.at[k + 1], ssem, peer)

    def stage_compress(u):
        ch = lax.rem(u, chunks)
        pl.when(u == 0)(lambda: arrive(comp, comp_sem))
        arrive(yrecv.at[u], y_sem.at[u])
        for d in (2, 1, 3, 0):
            j = other(my_z, d)
            acc = jnp.dot(comp[ch * GROUP + j], yrecv[u, j], preferred_element_type=F32)
            if d:
                z1s[u, j], z1ss[u, j] = quantize(acc)
                copy_pair(
                    z1s.at[u, j], z1ss.at[u, j], z1r.at[u, my_z], z1rs.at[u, my_z],
                    5, z1_sem.at[0, u], z1_sem.at[1, u], z_dev(j),
                )
            else:
                z1r[u, my_z], z1rs[u, my_z] = quantize(acc)

    def factors(ch, mq, ms, fh, fl):
        for level in range(2):
            for pair, (lower, upper) in enumerate(pairs(level)):
                for half, b in enumerate((lower, upper)):
                    x = restore(mq[b, ch, level * 64 : (level + 1) * 64, :], ms[b, ch, level])
                    rows = slice(half * 64, (half + 1) * 64)
                    fh[ch, level, pair, rows], fl[ch, level, pair, rows] = split(x)

    def two_levels(u, ch, rq, rs, fh, fl, sq, ss):
        blocks = [restore(rq[u, b], rs[u, b]) for b in range(GROUP)]
        for level in range(2):
            new = list(blocks)
            for pair, (lower, upper) in enumerate(pairs(level)):
                both = jnp.concatenate([blocks[lower], blocks[upper]], axis=0)
                out = product(fh[ch, level, pair], fl[ch, level, pair], both)
                new[lower], new[upper] = out[:64], out[64:]
            blocks = new
        for b in range(GROUP):
            sq[u, b], ss[u, b] = quantize(blocks[b])

    def stage_low(u):
        ch = lax.rem(u, chunks)

        @pl.when(u == 0)
        def _():
            arrive(mzr, m_sem.at[0])
            arrive(mzrs, m_sem.at[1])

        pl.when(u < chunks)(lambda: factors(ch, mzr, mzrs, fzh, fzl))

        arrive(z1r.at[u, sent], z1_sem.at[0, u])
        arrive(z1rs.at[u, sent], z1_sem.at[1, u])
        two_levels(u, ch, z1r, z1rs, fzh, fzl, z2s, z2ss)
        for d in (2, 1, 3, 0):
            b = other(my_z, d)
            to = high_dev(my_z, b, ch)

            def go(peer, b=b, k=7 if d else 11):
                copy_pair(
                    z2s.at[u, b], z2ss.at[u, b], x1r.at[u, my_x], x1rs.at[u, my_x],
                    k, x1_sem.at[0, u], x1_sem.at[1, u], peer,
                )

            if d:
                go((w, to * GROUP + b))
            else:
                pl.when(to == my_x)(functools.partial(go, None))
                pl.when(to != my_x)(functools.partial(go, (w, to * GROUP + b)))

    def stage_high(u):
        ch = lax.rem(u, chunks)

        @pl.when(u == 0)
        def _():
            arrive(mxr, m_sem.at[2])
            arrive(mxrs, m_sem.at[3])

        pl.when(u < chunks)(lambda: factors(ch, mxr, mxrs, fxh, fxl))

        arrive(x1r.at[u], x1_sem.at[0, u])
        arrive(x1rs.at[u], x1_sem.at[1, u])
        two_levels(u, ch, x1r, x1rs, fxh, fxl, x2s, x2ss)
        mine = high_slot(ch)
        for d in (2, 1, 3, 0):
            j = other(my_x, d)
            copy_pair(
                x2s.at[u, j], x2ss.at[u, j], out_q.at[u, mine], out_s.at[u, mine],
                9, o_sem.at[0], o_sem.at[1], x_dev(j) if d else None,
            )

    shape = onehot.shape
    row, col = (lax.broadcasted_iota(I32, shape, d) for d in range(2))
    per_chunk = waves * GROUP
    slot = (row % per_chunk // GROUP) * (chunks * GROUP) + row // per_chunk * GROUP + row % GROUP
    onehot[...] = lax.dot_general(
        (col == slot).astype(BF16), (row == m_slot[...]).astype(BF16),
        (((1,), (1,)), ((), ())), preferred_element_type=F32,
    ).astype(BF16)
    arrive(gbuf.at[0], load_sem.at[0])

    def pick_first(l, _):
        pick(0, l)
        return 0

    lax.fori_loop(0, lats, pick_first, 0)
    arrange(0)
    pl.semaphore_wait(barrier, len(peers))
    send_wave(0)
    prepare_mix()
    send_mix()
    pick_next(0)

    def step(t, _):
        for lag, stage in (
            (LEAD + 2 * LAG, stage_high),
            (LEAD + LAG, stage_low),
            (LEAD, stage_compress),
            (0, stage_gather),
        ):
            u = t - lag
            pl.when((u >= 0) & (u < units))(functools.partial(stage, u))
        return 0

    lax.fori_loop(1, units + LEAD + 2 * LAG, step, 0)

    arrive(out_q, o_sem.at[0])
    arrive(out_s, o_sem.at[1])
    arrive(ysend.at[:, pl.ds(0, (waves - 1) * GROUP)], send_sem.at[0])
    for k, ref in enumerate((mzs, mxs, mzss, mxss)):
        arrive(ref.at[sent], send_sem.at[1 + k])
    for k, ref in enumerate((z1s, z1ss)):
        arrive(ref.at[:, sent], send_sem.at[5 + k])
    for k, ref in enumerate((z2s, z2ss)):
        arrive(ref.at[:, sent], send_sem.at[7 + k])
    for k, ref in enumerate((x2s, x2ss)):
        arrive(ref.at[:, sent], send_sem.at[9 + k])
    far = lax.rem(my_x, 2) == 1
    for k, ref in enumerate((z2s, z2ss)):
        pl.when(far)(lambda k=k, ref=ref: arrive(ref.at[:, 0], send_sem.at[11 + k]))
        half = ref.at[pl.ds(0, units // 2), 0]
        pl.when(jnp.logical_not(far))(lambda k=k, half=half: arrive(half, send_sem.at[11 + k]))


def exchange(m_slot, comp, grid, mix, waves):
    lats, all_slots, cols = grid.shape
    slots, rank, width = comp.shape
    n_cb = cols // CB
    chunks = slots // GROUP
    units = n_cb * chunks
    parts = (units, GROUP, rank, CB)
    scales = (units, GROUP, 1, CB)
    mq = (GROUP, chunks, 2 * rank, 2 * rank)
    ms = (GROUP, chunks, 2, 1, 2 * rank)
    vmem = pltpu.VMEM
    any_spec = pl.BlockSpec(memory_space=pl.ANY)
    return pl.pallas_call(
        exchange_kernel,
        out_shape=(jax.ShapeDtypeStruct(parts, I16), jax.ShapeDtypeStruct(scales, F32)),
        in_specs=[
            pl.BlockSpec(memory_space=pltpu.VMEM),
            any_spec,
            any_spec,
            any_spec,
        ],
        out_specs=(any_spec, any_spec),
        scratch_shapes=[
            vmem((n_cb, lats, all_slots, CB), BF16),
            vmem((2, lats, all_slots, CB), F32),
            vmem((units, waves * GROUP, lats, CB), BF16),
            vmem((units, GROUP, width, CB), BF16),
            vmem(mq, I16), vmem(ms, F32), vmem(mq, I16), vmem(ms, F32),
            vmem(mq, I16), vmem(ms, F32), vmem(mq, I16), vmem(ms, F32),
            *[vmem((chunks, 2, 2, 2 * rank, 2 * rank), BF16)] * 4,
            vmem(parts, I16), vmem(scales, F32), vmem(parts, I16), vmem(scales, F32),
            vmem(parts, I16), vmem(scales, F32),
            vmem(parts, I16), vmem(scales, F32),
            vmem(parts, I16), vmem(scales, F32),
            vmem((all_slots, all_slots), BF16),
            vmem(comp.shape, BF16),
            pltpu.SemaphoreType.DMA((n_cb,)),
            pltpu.SemaphoreType.DMA,
            pltpu.SemaphoreType.DMA,
            pltpu.SemaphoreType.DMA((13,)),
            pltpu.SemaphoreType.DMA((units,)),
            pltpu.SemaphoreType.DMA((4,)),
            pltpu.SemaphoreType.DMA((2, units)),
            pltpu.SemaphoreType.DMA((2, units)),
            pltpu.SemaphoreType.DMA((2,)),
        ],
        compiler_params=pltpu.CompilerParams(
            collective_id=0, has_side_effects=True, vmem_limit_bytes=60 * 2**20
        ),
        name="exchange",
    )(m_slot[None, :], comp, grid, mix)


def expand_kernel(m_slot, q_hbm, s_hbm, e_ref, out_hbm, q_ref, s_ref, held, q_sem, s_sem, out_sem):
    degrees = e_ref.shape[2]
    pieces = held.shape[0]
    per = q_hbm.shape[0] // pieces
    groups = e_ref.shape[0] // (per * GROUP)
    for p in range(pieces):
        part = pl.ds(p * per, per)
        pltpu.make_async_copy(q_hbm.at[part], q_ref.at[part], q_sem.at[p]).start()
    pltpu.make_async_copy(s_hbm, s_ref, s_sem).start()
    first = lax.axis_index("fly") * degrees
    base = lax.axis_index("wave") * e_ref.shape[0]
    degree = first + lax.broadcasted_iota(I32, (degrees, CB), 0)
    dot = functools.partial(
        lax.dot_general,
        dimension_numbers=(((0,), (0,)), ((), ())),
        preferred_element_type=F32,
    )

    def out_copy(p, i):
        cb, g = p // groups, lax.rem(p, groups)
        rows = pl.ds(i * (degrees // SPLIT), degrees // SPLIT)
        slots = pl.ds(pl.multiple_of(g * 8, 8), 8)
        cols = pl.ds(pl.multiple_of(cb * CB, CB), CB)
        return pltpu.make_async_copy(held.at[p, rows], out_hbm.at[rows, slots, cols], out_sem)

    pltpu.make_async_copy(s_hbm, s_ref, s_sem).wait()

    def piece(p, _):
        part = pl.ds(p * per, per)
        pltpu.make_async_copy(q_hbm.at[part], q_ref.at[part], q_sem.at[p]).wait()
        g = lax.rem(p, groups)
        vals = []
        for i in range(8):
            slot = g * 8 + i
            u, j = p * per + i // GROUP, i % GROUP
            eh, el = split(e_ref[slot])
            qh, ql = split(q_ref[u, j].astype(I32).astype(F32))
            val = dot(jnp.concatenate([eh, eh, el], axis=0), jnp.concatenate([qh, ql, qh], axis=0))
            val = val * s_ref[u, j]
            vals.append(jnp.where(degree >= m_slot[base + slot], val, 0.0))
        for c in range(CB // 128):
            cols = slice(c * 128, (c + 1) * 128)
            held[p, :, :, cols] = pltpu.einshape("sdc->dsc", jnp.stack([v[:, cols] for v in vals]))
        for i in range(SPLIT):
            out_copy(p, i).start()
        return 0

    lax.fori_loop(0, pieces, piece, 0)
    pltpu.make_async_copy(held, held, out_sem).wait()


def expand_out(m_slot, q, s, exp_t):
    units, _, rank, _ = q.shape
    slots, _, degrees = exp_t.shape
    n_cb = units * GROUP // slots
    pieces = n_cb * slots // 8
    return pl.pallas_call(
        expand_kernel,
        out_shape=jax.ShapeDtypeStruct((degrees, slots, n_cb * CB), F32),
        in_specs=[
            pl.BlockSpec(memory_space=pltpu.SMEM),
            pl.BlockSpec(memory_space=pl.ANY),
            pl.BlockSpec(memory_space=pl.ANY),
            pl.BlockSpec(memory_space=pltpu.VMEM),
        ],
        out_specs=pl.BlockSpec(memory_space=pl.ANY),
        scratch_shapes=[
            pltpu.VMEM(q.shape, I16),
            pltpu.VMEM(s.shape, F32),
            pltpu.VMEM((pieces, degrees, 8, CB), F32),
            pltpu.SemaphoreType.DMA((pieces,)),
            pltpu.SemaphoreType.DMA,
            pltpu.SemaphoreType.DMA,
        ],
        compiler_params=pltpu.CompilerParams(vmem_limit_bytes=60 * 2**20),
        name="expand_out",
    )(m_slot, q, s, exp_t)


def on_device(grid_fourier, m_slot, compress, mix, expand):
    comp = jnp.transpose(compress, (1, 2, 0))
    exp_t = jnp.transpose(expand, (1, 2, 0))
    waves = lax.axis_size("wave")
    q, s = exchange(m_slot, comp, grid_fourier, mix[0], waves)
    return expand_out(m_slot, q, s, exp_t)


def solution(mesh):
    in_specs = (
        P(("fly", "wave"), None, None),
        P(),
        P("fly", "wave", None),
        P("fly", "wave", None, None),
        P("fly", "wave", None),
    )
    return jax.shard_map(
        on_device, mesh=mesh, in_specs=in_specs, out_specs=P("fly", "wave", None),
        check_vma=False,
    )
```

```python
import functools

import jax
import jax.numpy as jnp
from jax import lax
from jax.experimental import pallas as pl
from jax.experimental.pallas import tpu as pltpu
from jax.sharding import PartitionSpec as P

MESH = pl.DeviceIdType.MESH
F32, BF16, I16, I32 = jnp.float32, jnp.bfloat16, jnp.int16, jnp.int32

CB = 128
GROUP = 4
HALVES = 2
UNIT = GROUP * HALVES
WIDE = 3
LAG = 3
LEAD = 4
QMAX = 32766.0


def quantize(x):
    largest = jnp.maximum(jnp.max(jnp.abs(x), axis=0, keepdims=True), 1e-30)
    q = jnp.round(x * (QMAX / largest)).astype(I32).astype(I16)
    return q, largest * (1.0 / QMAX)


def restore(q, scale):
    return q.astype(I32).astype(F32) * scale


def split(x):
    high = x.astype(BF16)
    return high, (x - high.astype(F32)).astype(BF16)


def product(ah, al, b):
    bh, bl = split(b)
    left = jnp.concatenate([ah, ah, al], axis=1)
    return jnp.dot(left, jnp.concatenate([bh, bl, bh], axis=0), preferred_element_type=F32)


def pairs(level):
    return [(b, b | 1 << level) for b in range(GROUP) if not b >> level & 1]


def exchange_kernel(
    m_slot, comp_hbm, grid, mix, out_q, out_s,
    gbuf, flat, ysend, yrecv, mixf,
    mzs, mzss, mzr, mzrs, mxs, mxss, mxr, mxrs, fzh, fzl, fxh, fxl,
    z1s, z1ss, z1r, z1rs, z2s, z2ss, x1r, x1rs, x2s, x2ss,
    onehot, comp, load_sem, comp_sem, mix_sem, send_sem, y_sem, m_sem, z1_sem, x1_sem, o_sem,
):
    units, lats = ysend.shape[0], ysend.shape[2]
    waves = ysend.shape[1] // UNIT
    n_cb = gbuf.shape[0]
    chunks = units // n_cb
    w, f = lax.axis_index("wave"), lax.axis_index("fly")
    my_x, my_z = f // GROUP, lax.rem(f, GROUP)

    def z_dev(j):
        return (w, my_x * GROUP + j)

    def x_dev(j):
        return (w, j * GROUP + my_z)

    def other(mine, d):
        return lax.rem(mine + d, GROUP)

    for cb in range(n_cb):
        pltpu.make_async_copy(
            grid.at[:, :, pl.ds(cb * CB, CB)], gbuf.at[cb], load_sem.at[cb]
        ).start()
    pltpu.make_async_copy(comp_hbm, comp, comp_sem).start()
    pltpu.make_async_copy(mix, mixf, mix_sem).start()

    barrier = pltpu.get_barrier_semaphore()
    peers = [(lax.rem(w + d, waves), f) for d in range(1, waves)]
    peers += [(w, lax.rem(f + d, GROUP * GROUP)) for d in range(1, GROUP * GROUP)]
    for peer in peers:
        pl.semaphore_signal(barrier, inc=1, device_id=peer, device_id_type=MESH)

    sent = pl.ds(0, GROUP - 1)

    def push(src, dst, send, recv, peer):
        pltpu.make_async_remote_copy(
            src_ref=src, dst_ref=dst, send_sem=send, recv_sem=recv,
            device_id=peer, device_id_type=MESH,
        ).start()

    def arrive(ref, sem):
        pltpu.make_async_copy(ref, ref, sem).wait()

    def pick(cb, l):
        flat[lax.rem(cb, 2), l] = jnp.dot(onehot[...], gbuf[cb, l], preferred_element_type=F32)

    def arrange(u):
        cb, ch = u // chunks, lax.rem(u, chunks)
        for r in range(0, waves * UNIT, 8):
            rows = pl.ds(pl.multiple_of(ch * (waves * UNIT) + r, 8), 8)
            for c in range(0, CB, 128):
                x = flat[lax.rem(cb, 2), :, rows, c : c + 128]
                ysend[u, r : r + 8, :, c : c + 128] = pltpu.einshape("lsc->slc", x).astype(BF16)

    def send_wave(u):
        dst = yrecv.at[u, :, pl.ds(pl.multiple_of(w * lats, lats), lats), :]
        for d in range(1, waves):
            to = lax.rem(w + d, waves)
            push(ysend.at[u, pl.ds(to * UNIT, UNIT)], dst, send_sem.at[0], y_sem.at[u], (to, f))
        pltpu.make_async_copy(ysend.at[u, pl.ds(w * UNIT, UNIT)], dst, y_sem.at[u]).start()

    def stage_gather(u):
        arrange(u)
        send_wave(u)
        pick_next(u)

    def pick_next(u):
        cb, ch = u // chunks, lax.rem(u, chunks)
        for k in range(1, n_cb):
            first = (k - 1) * chunks
            pl.when(u == first)(lambda k=k: arrive(gbuf.at[k], load_sem.at[k]))

        @pl.when(cb + 1 < n_cb)
        def _():
            for i in range(lats // chunks):
                pick(cb + 1, ch * (lats // chunks) + i)

    def high_dev(j, b, half):
        return lax.rem(j + b + 2 * half, GROUP)

    def prepare_mix():
        arrive(mixf, mix_sem)

        def one(ch, _):
            for j in range(GROUP):
                for level in range(4):
                    q, s = quantize(mixf[ch * GROUP + j, level * 64 : (level + 1) * 64, :])
                    if level < 2:
                        sq, ss, to = mzs, mzss, j
                    else:
                        sq, ss, to = mxs, mxss, high_dev(j, my_z, lax.rem(ch, HALVES))
                    sq[to, ch, (level % 2) * 64 : (level % 2 + 1) * 64, :] = q
                    ss[to, ch, level % 2] = s
            return 0

        lax.fori_loop(0, chunks * HALVES, one, 0)

    def send_mix():
        for mine, dev, sq, ss, rq, rs, k in (
            (my_z, z_dev, mzs, mzss, mzr, mzrs, 0),
            (my_x, x_dev, mxs, mxss, mxr, mxrs, 1),
        ):
            for d in range(1, GROUP):
                j = other(mine, d)
                push(sq.at[j], rq.at[mine], send_sem.at[1 + k], m_sem.at[2 * k], dev(j))
                push(ss.at[j], rs.at[mine], send_sem.at[3 + k], m_sem.at[2 * k + 1], dev(j))
            pltpu.make_async_copy(sq.at[mine], rq.at[mine], m_sem.at[2 * k]).start()
            pltpu.make_async_copy(ss.at[mine], rs.at[mine], m_sem.at[2 * k + 1]).start()

    def copy_pair(sq, ss, dq, ds, k, qsem, ssem, peer):
        if peer is None:
            pltpu.make_async_copy(sq, dq, qsem).start()
            pltpu.make_async_copy(ss, ds, ssem).start()
        else:
            push(sq, dq, send_sem.at[k], qsem, peer)
            push(ss, ds, send_sem.at[k + 1], ssem, peer)

    def stage_compress(u):
        ch = lax.rem(u, chunks)
        pl.when(u == 0)(lambda: arrive(comp, comp_sem))
        arrive(yrecv.at[u], y_sem.at[u])
        for d in (2, 1, 3, 0):
            j = other(my_z, d)
            for half in range(HALVES):
                i = half * GROUP + j
                acc = jnp.dot(comp[ch * UNIT + i], yrecv[u, i], preferred_element_type=F32)
                if d:
                    z1s[u, j, half], z1ss[u, j, half] = quantize(acc)
                else:
                    z1r[u, my_z, half], z1rs[u, my_z, half] = quantize(acc)
            if d:
                copy_pair(
                    z1s.at[u, j], z1ss.at[u, j], z1r.at[u, my_z], z1rs.at[u, my_z],
                    5, z1_sem.at[0, u], z1_sem.at[1, u], z_dev(j),
                )

    def factors(c, mq, ms, fh, fl):
        for level in range(2):
            for pair, (lower, upper) in enumerate(pairs(level)):
                for half, b in enumerate((lower, upper)):
                    x = restore(mq[b, c, level * 64 : (level + 1) * 64, :], ms[b, c, level])
                    rows = slice(half * 64, (half + 1) * 64)
                    fh[c, level, pair, rows], fl[c, level, pair, rows] = split(x)

    def two_levels(u, ch, rq, rs, fh, fl, sq, ss):
        for half in range(HALVES):
            c = ch * HALVES + half
            blocks = [restore(rq[u, b, half], rs[u, b, half]) for b in range(GROUP)]
            for level in range(2):
                new = list(blocks)
                for pair, (lower, upper) in enumerate(pairs(level)):
                    both = jnp.concatenate([blocks[lower], blocks[upper]], axis=0)
                    out = product(fh[c, level, pair], fl[c, level, pair], both)
                    new[lower], new[upper] = out[:64], out[64:]
                blocks = new
            for b in range(GROUP):
                sq[u, b, half], ss[u, b, half] = quantize(blocks[b])

    def stage_low(u):
        ch = lax.rem(u, chunks)

        @pl.when(u == 0)
        def _():
            arrive(mzr, m_sem.at[0])
            arrive(mzrs, m_sem.at[1])

        @pl.when(u < chunks)
        def _():
            for half in range(HALVES):
                factors(ch * HALVES + half, mzr, mzrs, fzh, fzl)


        arrive(z1r.at[u, sent], z1_sem.at[0, u])
        arrive(z1rs.at[u, sent], z1_sem.at[1, u])
        two_levels(u, ch, z1r, z1rs, fzh, fzl, z2s, z2ss)
        for d in (2, 1, 3, 0):
            b = other(my_z, d)
            for half in range(HALVES):
                to = high_dev(my_z, b, half)

                def go(peer, b=b, half=half, k=7 if d else 11):
                    copy_pair(
                        z2s.at[u, b, half], z2ss.at[u, b, half],
                        x1r.at[u, my_x, half], x1rs.at[u, my_x, half],
                        k, x1_sem.at[0, u], x1_sem.at[1, u], peer,
                    )

                if d:
                    go((w, to * GROUP + b))
                else:
                    pl.when(to == my_x)(functools.partial(go, None))
                    pl.when(to != my_x)(functools.partial(go, (w, to * GROUP + b)))

    def stage_high(u):
        ch = lax.rem(u, chunks)

        @pl.when(u == 0)
        def _():
            arrive(mxr, m_sem.at[2])
            arrive(mxrs, m_sem.at[3])

        @pl.when(u < chunks)
        def _():
            for half in range(HALVES):
                factors(ch * HALVES + half, mxr, mxrs, fxh, fxl)


        arrive(x1r.at[u], x1_sem.at[0, u])
        arrive(x1rs.at[u], x1_sem.at[1, u])
        two_levels(u, ch, x1r, x1rs, fxh, fxl, x2s, x2ss)
        for d in (2, 1, 3, 0):
            j = other(my_x, d)
            copy_pair(
                x2s.at[u, j], x2ss.at[u, j], out_q.at[u, my_x], out_s.at[u, my_x],
                9, o_sem.at[0], o_sem.at[1], x_dev(j) if d else None,
            )

    shape = onehot.shape
    row, col = (lax.broadcasted_iota(I32, shape, d) for d in range(2))
    per_chunk = waves * UNIT
    slot = (row % per_chunk // UNIT) * (chunks * UNIT) + row // per_chunk * UNIT + row % UNIT
    onehot[...] = lax.dot_general(
        (col == slot).astype(BF16), (row == m_slot[...]).astype(BF16),
        (((1,), (1,)), ((), ())), preferred_element_type=F32,
    ).astype(BF16)
    arrive(gbuf.at[0], load_sem.at[0])

    def pick_first(l, _):
        pick(0, l)
        return 0

    lax.fori_loop(0, lats, pick_first, 0)
    arrange(0)
    pl.semaphore_wait(barrier, len(peers))
    send_wave(0)
    prepare_mix()
    send_mix()
    pick_next(0)

    def step(t, _):
        for lag, stage in (
            (LEAD + 2 * LAG, stage_high),
            (LEAD + LAG, stage_low),
            (LEAD, stage_compress),
            (0, stage_gather),
        ):
            u = t - lag
            pl.when((u >= 0) & (u < units))(functools.partial(stage, u))
        return 0

    lax.fori_loop(1, units + LEAD + 2 * LAG, step, 0)

    arrive(out_q, o_sem.at[0])
    arrive(out_s, o_sem.at[1])
    arrive(ysend.at[:, pl.ds(0, (waves - 1) * UNIT)], send_sem.at[0])
    for k, ref in enumerate((mzs, mxs, mzss, mxss)):
        arrive(ref.at[sent], send_sem.at[1 + k])
    for k, ref in enumerate((z1s, z1ss)):
        arrive(ref.at[:, sent], send_sem.at[5 + k])
    for k, ref in enumerate((z2s, z2ss)):
        arrive(ref.at[:, sent], send_sem.at[7 + k])
    for k, ref in enumerate((x2s, x2ss)):
        arrive(ref.at[:, sent], send_sem.at[9 + k])
    far = lax.rem(my_x, 2) == 1
    for k, ref in enumerate((z2s, z2ss)):
        pl.when(far)(lambda k=k, ref=ref: arrive(ref.at[:, 0], send_sem.at[11 + k]))
        half = ref.at[:, 0, 0]
        pl.when(jnp.logical_not(far))(lambda k=k, half=half: arrive(half, send_sem.at[11 + k]))


def exchange(m_slot, comp, grid, mix, waves):
    lats, all_slots, cols = grid.shape
    slots, rank, width = comp.shape
    n_cb = cols // CB
    chunks = slots // UNIT
    units = n_cb * chunks
    parts = (units, GROUP, HALVES, rank, CB)
    scales = (units, GROUP, HALVES, 1, CB)
    mq = (GROUP, chunks * HALVES, 2 * rank, 2 * rank)
    ms = (GROUP, chunks * HALVES, 2, 1, 2 * rank)
    vmem = pltpu.VMEM
    any_spec = pl.BlockSpec(memory_space=pl.ANY)
    return pl.pallas_call(
        exchange_kernel,
        out_shape=(jax.ShapeDtypeStruct(parts, I16), jax.ShapeDtypeStruct(scales, F32)),
        in_specs=[
            pl.BlockSpec(memory_space=pltpu.VMEM),
            any_spec,
            any_spec,
            any_spec,
        ],
        out_specs=(any_spec, any_spec),
        scratch_shapes=[
            vmem((n_cb, lats, all_slots, CB), BF16),
            vmem((2, lats, all_slots, CB), F32),
            vmem((units, waves * UNIT, lats, CB), BF16),
            vmem((units, UNIT, width, CB), BF16),
            vmem(mix.shape, F32),
            vmem(mq, I16), vmem(ms, F32), vmem(mq, I16), vmem(ms, F32),
            vmem(mq, I16), vmem(ms, F32), vmem(mq, I16), vmem(ms, F32),
            *[vmem((chunks * HALVES, 2, 2, 2 * rank, 2 * rank), BF16)] * 4,
            vmem(parts, I16), vmem(scales, F32), vmem(parts, I16), vmem(scales, F32),
            vmem(parts, I16), vmem(scales, F32),
            vmem(parts, I16), vmem(scales, F32),
            vmem(parts, I16), vmem(scales, F32),
            vmem((all_slots, all_slots), BF16),
            vmem(comp.shape, BF16),
            pltpu.SemaphoreType.DMA((n_cb,)),
            pltpu.SemaphoreType.DMA,
            pltpu.SemaphoreType.DMA,
            pltpu.SemaphoreType.DMA((13,)),
            pltpu.SemaphoreType.DMA((units,)),
            pltpu.SemaphoreType.DMA((4,)),
            pltpu.SemaphoreType.DMA((2, units)),
            pltpu.SemaphoreType.DMA((2, units)),
            pltpu.SemaphoreType.DMA((2,)),
        ],
        compiler_params=pltpu.CompilerParams(
            collective_id=0, has_side_effects=True, vmem_limit_bytes=60 * 2**20
        ),
        name="exchange",
    )(m_slot[None, :], comp, grid, mix)


def expand_kernel(m_slot, q_hbm, s_hbm, e_ref, out_hbm, q_ref, s_ref, held, q_sem, s_sem, out_sem):
    slots, _, degrees = e_ref.shape
    chunks = slots // UNIT
    cols = WIDE * CB

    def load(k):
        part = pl.ds(k * chunks, chunks)
        return pltpu.make_async_copy(q_hbm.at[part], q_ref.at[part], q_sem.at[k])

    scales = pltpu.make_async_copy(s_hbm, s_ref, s_sem)
    for k in range(WIDE):
        load(k).start()
    scales.start()
    for k in range(WIDE, q_ref.shape[0] // chunks):
        load(k).start()
    my_z = lax.rem(lax.axis_index("fly"), GROUP)
    first = lax.axis_index("fly") * degrees
    base = lax.axis_index("wave") * slots
    degree = first + lax.broadcasted_iota(I32, (degrees, CB), 0)
    dot = functools.partial(
        lax.dot_general,
        dimension_numbers=(((0,), (0,)), ((), ())),
        preferred_element_type=F32,
    )
    scales.wait()

    def piece(p, _):
        block, ch = p // chunks, lax.rem(p, chunks)

        @pl.when(ch == 0)
        def _():
            for k in range(WIDE):
                load(block * WIDE + k).wait()

        left = []
        for i in range(UNIT):
            eh, el = split(e_ref[ch * UNIT + i])
            left.append(jnp.concatenate([eh, eh, el], axis=0))
        for k in range(WIDE):
            u = (block * WIDE + k) * chunks + ch
            vals = []
            for i in range(UNIT):
                half, j = i // GROUP, i % GROUP
                x = lax.rem(j + my_z + 2 * half, GROUP)
                qh, ql = split(q_ref[u, x, half].astype(I32).astype(F32))
                val = dot(left[i], jnp.concatenate([qh, ql, qh], axis=0)) * s_ref[u, x, half]
                vals.append(jnp.where(degree >= m_slot[base + ch * UNIT + i], val, 0.0))
            held[p, :, :, k * CB : (k + 1) * CB] = pltpu.einshape("sdc->dsc", jnp.stack(vals))
        to = out_hbm.at[
            :,
            pl.ds(pl.multiple_of(ch * UNIT, UNIT), UNIT),
            pl.ds(pl.multiple_of(block * cols, cols), cols),
        ]
        pltpu.make_async_copy(held.at[p], to, out_sem).start()
        return 0

    lax.fori_loop(0, held.shape[0], piece, 0)
    pltpu.make_async_copy(held, held, out_sem).wait()


def expand_out(m_slot, q, s, exp_t):
    units = q.shape[0]
    slots, _, degrees = exp_t.shape
    n_cb = units * UNIT // slots
    return pl.pallas_call(
        expand_kernel,
        out_shape=jax.ShapeDtypeStruct((degrees, slots, n_cb * CB), F32),
        in_specs=[
            pl.BlockSpec(memory_space=pltpu.SMEM),
            pl.BlockSpec(memory_space=pl.ANY),
            pl.BlockSpec(memory_space=pl.ANY),
            pl.BlockSpec(memory_space=pltpu.VMEM),
        ],
        out_specs=pl.BlockSpec(memory_space=pl.ANY),
        scratch_shapes=[
            pltpu.VMEM(q.shape, I16),
            pltpu.VMEM(s.shape, F32),
            pltpu.VMEM((units // WIDE, degrees, UNIT, WIDE * CB), F32),
            pltpu.SemaphoreType.DMA((n_cb,)),
            pltpu.SemaphoreType.DMA,
            pltpu.SemaphoreType.DMA,
        ],
        compiler_params=pltpu.CompilerParams(vmem_limit_bytes=60 * 2**20),
        name="expand_out",
    )(m_slot, q, s, exp_t)


def on_device(grid_fourier, m_slot, compress, mix, expand):
    comp = jnp.transpose(compress, (1, 2, 0))
    exp_t = jnp.transpose(expand, (1, 2, 0))
    waves = lax.axis_size("wave")
    q, s = exchange(m_slot, comp, grid_fourier, mix[0], waves)
    return expand_out(m_slot, q, s, exp_t)


def solution(mesh):
    in_specs = (
        P(("fly", "wave"), None, None),
        P(),
        P("fly", "wave", None),
        P("fly", "wave", None, None),
        P("fly", "wave", None),
    )
    return jax.shard_map(
        on_device, mesh=mesh, in_specs=in_specs, out_specs=P("fly", "wave", None),
        check_vma=False,
    )
```

```python
import functools

import jax
import jax.numpy as jnp
from jax import lax
from jax.experimental import pallas as pl
from jax.experimental.pallas import tpu as pltpu
from jax.sharding import PartitionSpec as P

MESH = pl.DeviceIdType.MESH
F32, BF16, I16, I32 = jnp.float32, jnp.bfloat16, jnp.int16, jnp.int32

CB = 128
GROUP = 4
HALVES = 2
UNIT = GROUP * HALVES
WIDE = 3
LAG = 3
LEAD = 4
QMAX = 32766.0


def quantize(x):
    largest = jnp.maximum(jnp.max(jnp.abs(x), axis=0, keepdims=True), 1e-30)
    q = jnp.round(x * (QMAX / largest)).astype(I32).astype(I16)
    return q, largest * (1.0 / QMAX)


def restore(q, scale):
    return q.astype(I32).astype(F32) * scale


def split(x):
    high = x.astype(BF16)
    return high, (x - high.astype(F32)).astype(BF16)


def product(ah, al, b):
    bh, bl = split(b)
    left = jnp.concatenate([ah, ah, al], axis=1)
    return jnp.dot(left, jnp.concatenate([bh, bl, bh], axis=0), preferred_element_type=F32)


def pairs(level):
    return [(b, b | 1 << level) for b in range(GROUP) if not b >> level & 1]


def exchange_kernel(
    m_slot, comp_hbm, grid, mix, out_q, out_s,
    gbuf, flat, ysend, yrecv, mixf,
    mzs, mzss, mzr, mzrs, mxs, mxss, mxr, mxrs, fzh, fzl, fxh, fxl,
    z1s, z1ss, z1r, z1rs, z2s, z2ss, x1r, x1rs, x2s, x2ss,
    onehot, comp, load_sem, comp_sem, mix_sem, send_sem, y_sem, m_sem, z1_sem, x1_sem, o_sem,
):
    units, lats = ysend.shape[0], ysend.shape[2]
    waves = ysend.shape[1] // UNIT
    n_cb = gbuf.shape[0]
    chunks = units // n_cb
    w, f = lax.axis_index("wave"), lax.axis_index("fly")
    my_x, my_z = f // GROUP, lax.rem(f, GROUP)

    def z_dev(j):
        return (w, my_x * GROUP + j)

    def x_dev(j):
        return (w, j * GROUP + my_z)

    def other(mine, d):
        return lax.rem(mine + d, GROUP)

    for cb in range(n_cb):
        pltpu.make_async_copy(
            grid.at[:, :, pl.ds(cb * CB, CB)], gbuf.at[cb], load_sem.at[cb]
        ).start()
    pltpu.make_async_copy(comp_hbm, comp, comp_sem).start()
    pltpu.make_async_copy(mix, mixf, mix_sem).start()

    barrier = pltpu.get_barrier_semaphore()
    peers = [(lax.rem(w + d, waves), f) for d in range(1, waves)]
    peers += [(w, lax.rem(f + d, GROUP * GROUP)) for d in range(1, GROUP * GROUP)]
    for peer in peers:
        pl.semaphore_signal(barrier, inc=1, device_id=peer, device_id_type=MESH)

    sent = pl.ds(0, GROUP - 1)

    def push(src, dst, send, recv, peer):
        pltpu.make_async_remote_copy(
            src_ref=src, dst_ref=dst, send_sem=send, recv_sem=recv,
            device_id=peer, device_id_type=MESH,
        ).start()

    def arrive(ref, sem):
        pltpu.make_async_copy(ref, ref, sem).wait()

    def pick(cb, l):
        flat[lax.rem(cb, 2), l] = jnp.dot(onehot[...], gbuf[cb, l], preferred_element_type=F32)

    def arrange(u):
        cb, ch = u // chunks, lax.rem(u, chunks)
        for r in range(0, waves * UNIT, 8):
            rows = pl.ds(pl.multiple_of(ch * (waves * UNIT) + r, 8), 8)
            for c in range(0, CB, 128):
                x = flat[lax.rem(cb, 2), :, rows, c : c + 128]
                ysend[u, r : r + 8, :, c : c + 128] = pltpu.einshape("lsc->slc", x).astype(BF16)

    def send_wave(u):
        dst = yrecv.at[u, :, pl.ds(pl.multiple_of(w * lats, lats), lats), :]
        for d in range(1, waves):
            to = lax.rem(w + d, waves)
            push(ysend.at[u, pl.ds(to * UNIT, UNIT)], dst, send_sem.at[0], y_sem.at[u], (to, f))
        pltpu.make_async_copy(ysend.at[u, pl.ds(w * UNIT, UNIT)], dst, y_sem.at[u]).start()

    def stage_gather(u):
        arrange(u)
        send_wave(u)
        pick_next(u)

    def pick_next(u):
        cb, ch = u // chunks, lax.rem(u, chunks)
        for k in range(1, n_cb):
            first = (k - 1) * chunks
            pl.when(u == first)(lambda k=k: arrive(gbuf.at[k], load_sem.at[k]))

        @pl.when(cb + 1 < n_cb)
        def _():
            for i in range(lats // chunks):
                pick(cb + 1, ch * (lats // chunks) + i)

    def high_dev(j, b, half):
        return lax.rem(j + b + 2 * half, GROUP)

    def prepare_mix():
        arrive(mixf, mix_sem)

        def one(ch, _):
            for j in range(GROUP):
                for level in range(4):
                    q, s = quantize(mixf[ch * GROUP + j, level * 64 : (level + 1) * 64, :])
                    if level < 2:
                        sq, ss, to = mzs, mzss, j
                    else:
                        sq, ss, to = mxs, mxss, high_dev(j, my_z, lax.rem(ch, HALVES))
                    sq[to, ch, (level % 2) * 64 : (level % 2 + 1) * 64, :] = q
                    ss[to, ch, level % 2] = s
            return 0

        lax.fori_loop(0, chunks * HALVES, one, 0)

    def send_mix():
        for mine, dev, sq, ss, rq, rs, k in (
            (my_z, z_dev, mzs, mzss, mzr, mzrs, 0),
            (my_x, x_dev, mxs, mxss, mxr, mxrs, 1),
        ):
            for d in range(1, GROUP):
                j = other(mine, d)
                push(sq.at[j], rq.at[mine], send_sem.at[1 + k], m_sem.at[2 * k], dev(j))
                push(ss.at[j], rs.at[mine], send_sem.at[3 + k], m_sem.at[2 * k + 1], dev(j))
            pltpu.make_async_copy(sq.at[mine], rq.at[mine], m_sem.at[2 * k]).start()
            pltpu.make_async_copy(ss.at[mine], rs.at[mine], m_sem.at[2 * k + 1]).start()

    def copy_pair(sq, ss, dq, ds, k, qsem, ssem, peer):
        if peer is None:
            pltpu.make_async_copy(sq, dq, qsem).start()
            pltpu.make_async_copy(ss, ds, ssem).start()
        else:
            push(sq, dq, send_sem.at[k], qsem, peer)
            push(ss, ds, send_sem.at[k + 1], ssem, peer)

    def stage_compress(u):
        ch = lax.rem(u, chunks)
        pl.when(u == 0)(lambda: arrive(comp, comp_sem))
        arrive(yrecv.at[u], y_sem.at[u])
        for d in (2, 1, 3, 0):
            j = other(my_z, d)
            for half in range(HALVES):
                i = half * GROUP + j
                acc = jnp.dot(comp[ch * UNIT + i], yrecv[u, i], preferred_element_type=F32)
                if d:
                    z1s[u, j, half], z1ss[u, j, half] = quantize(acc)
                else:
                    z1r[u, my_z, half], z1rs[u, my_z, half] = quantize(acc)
            if d:
                copy_pair(
                    z1s.at[u, j], z1ss.at[u, j], z1r.at[u, my_z], z1rs.at[u, my_z],
                    5, z1_sem.at[0, u], z1_sem.at[1, u], z_dev(j),
                )

    def factors(c, mq, ms, fh, fl):
        for level in range(2):
            for pair, (lower, upper) in enumerate(pairs(level)):
                for half, b in enumerate((lower, upper)):
                    x = restore(mq[b, c, level * 64 : (level + 1) * 64, :], ms[b, c, level])
                    rows = slice(half * 64, (half + 1) * 64)
                    fh[c, level, pair, rows], fl[c, level, pair, rows] = split(x)

    def two_levels(u, ch, rq, rs, fh, fl, sq, ss):
        for half in range(HALVES):
            c = ch * HALVES + half
            blocks = [restore(rq[u, b, half], rs[u, b, half]) for b in range(GROUP)]
            for level in range(2):
                new = list(blocks)
                for pair, (lower, upper) in enumerate(pairs(level)):
                    both = jnp.concatenate([blocks[lower], blocks[upper]], axis=0)
                    out = product(fh[c, level, pair], fl[c, level, pair], both)
                    new[lower], new[upper] = out[:64], out[64:]
                blocks = new
            for b in range(GROUP):
                sq[u, b, half], ss[u, b, half] = quantize(blocks[b])

    def stage_low(u):
        ch = lax.rem(u, chunks)

        @pl.when(u == 0)
        def _():
            arrive(mzr, m_sem.at[0])
            arrive(mzrs, m_sem.at[1])

        @pl.when(u < chunks)
        def _():
            for half in range(HALVES):
                factors(ch * HALVES + half, mzr, mzrs, fzh, fzl)


        arrive(z1r.at[u, sent], z1_sem.at[0, u])
        arrive(z1rs.at[u, sent], z1_sem.at[1, u])
        two_levels(u, ch, z1r, z1rs, fzh, fzl, z2s, z2ss)
        for d in (2, 1, 3, 0):
            b = other(my_z, d)
            for half in range(HALVES):
                to = high_dev(my_z, b, half)

                def go(peer, b=b, half=half, k=7 if d else 11):
                    copy_pair(
                        z2s.at[u, b, half], z2ss.at[u, b, half],
                        x1r.at[u, my_x, half], x1rs.at[u, my_x, half],
                        k, x1_sem.at[0, u], x1_sem.at[1, u], peer,
                    )

                if d:
                    go((w, to * GROUP + b))
                else:
                    pl.when(to == my_x)(functools.partial(go, None))
                    pl.when(to != my_x)(functools.partial(go, (w, to * GROUP + b)))

    def stage_high(u):
        ch = lax.rem(u, chunks)

        @pl.when(u == 0)
        def _():
            arrive(mxr, m_sem.at[2])
            arrive(mxrs, m_sem.at[3])

        @pl.when(u < chunks)
        def _():
            for half in range(HALVES):
                factors(ch * HALVES + half, mxr, mxrs, fxh, fxl)


        arrive(x1r.at[u], x1_sem.at[0, u])
        arrive(x1rs.at[u], x1_sem.at[1, u])
        two_levels(u, ch, x1r, x1rs, fxh, fxl, x2s, x2ss)
        for d in (2, 1, 3, 0):
            j = other(my_x, d)
            copy_pair(
                x2s.at[u, j], x2ss.at[u, j], out_q.at[u, my_x], out_s.at[u, my_x],
                9, o_sem.at[0], o_sem.at[1], x_dev(j) if d else None,
            )

    shape = onehot.shape
    row, col = (lax.broadcasted_iota(I32, shape, d) for d in range(2))
    per_chunk = waves * UNIT
    slot = (row % per_chunk // UNIT) * (chunks * UNIT) + row // per_chunk * UNIT + row % UNIT
    onehot[...] = lax.dot_general(
        (col == slot).astype(BF16), (row == m_slot[...]).astype(BF16),
        (((1,), (1,)), ((), ())), preferred_element_type=F32,
    ).astype(BF16)
    arrive(gbuf.at[0], load_sem.at[0])

    def pick_first(l, _):
        pick(0, l)
        return 0

    lax.fori_loop(0, lats, pick_first, 0)
    arrange(0)
    pl.semaphore_wait(barrier, len(peers))
    send_wave(0)
    prepare_mix()
    send_mix()
    pick_next(0)

    def step(t, _):
        for lag, stage in (
            (LEAD + 2 * LAG, stage_high),
            (LEAD + LAG, stage_low),
            (LEAD, stage_compress),
            (0, stage_gather),
        ):
            u = t - lag
            pl.when((u >= 0) & (u < units))(functools.partial(stage, u))
        return 0

    lax.fori_loop(1, units + LEAD + 2 * LAG, step, 0)

    arrive(out_q, o_sem.at[0])
    arrive(out_s, o_sem.at[1])
    arrive(ysend.at[:, pl.ds(0, (waves - 1) * UNIT)], send_sem.at[0])
    for k, ref in enumerate((mzs, mxs, mzss, mxss)):
        arrive(ref.at[sent], send_sem.at[1 + k])
    for k, ref in enumerate((z1s, z1ss)):
        arrive(ref.at[:, sent], send_sem.at[5 + k])
    for k, ref in enumerate((z2s, z2ss)):
        arrive(ref.at[:, sent], send_sem.at[7 + k])
    for k, ref in enumerate((x2s, x2ss)):
        arrive(ref.at[:, sent], send_sem.at[9 + k])
    far = lax.rem(my_x, 2) == 1
    for k, ref in enumerate((z2s, z2ss)):
        pl.when(far)(lambda k=k, ref=ref: arrive(ref.at[:, 0], send_sem.at[11 + k]))
        half = ref.at[:, 0, 0]
        pl.when(jnp.logical_not(far))(lambda k=k, half=half: arrive(half, send_sem.at[11 + k]))


def exchange(m_slot, comp, grid, mix, waves):
    lats, all_slots, cols = grid.shape
    slots, rank, width = comp.shape
    n_cb = cols // CB
    chunks = slots // UNIT
    units = n_cb * chunks
    parts = (units, GROUP, HALVES, rank, CB)
    scales = (units, GROUP, HALVES, 1, CB)
    mq = (GROUP, chunks * HALVES, 2 * rank, 2 * rank)
    ms = (GROUP, chunks * HALVES, 2, 1, 2 * rank)
    vmem = pltpu.VMEM
    any_spec = pl.BlockSpec(memory_space=pl.ANY)
    return pl.pallas_call(
        exchange_kernel,
        out_shape=(jax.ShapeDtypeStruct(parts, I16), jax.ShapeDtypeStruct(scales, F32)),
        in_specs=[
            pl.BlockSpec(memory_space=pltpu.VMEM),
            any_spec,
            any_spec,
            any_spec,
        ],
        out_specs=(any_spec, any_spec),
        scratch_shapes=[
            vmem((n_cb, lats, all_slots, CB), BF16),
            vmem((2, lats, all_slots, CB), F32),
            vmem((units, waves * UNIT, lats, CB), BF16),
            vmem((units, UNIT, width, CB), BF16),
            vmem(mix.shape, F32),
            vmem(mq, I16), vmem(ms, F32), vmem(mq, I16), vmem(ms, F32),
            vmem(mq, I16), vmem(ms, F32), vmem(mq, I16), vmem(ms, F32),
            *[vmem((chunks * HALVES, 2, 2, 2 * rank, 2 * rank), BF16)] * 4,
            vmem(parts, I16), vmem(scales, F32), vmem(parts, I16), vmem(scales, F32),
            vmem(parts, I16), vmem(scales, F32),
            vmem(parts, I16), vmem(scales, F32),
            vmem(parts, I16), vmem(scales, F32),
            vmem((all_slots, all_slots), BF16),
            vmem(comp.shape, BF16),
            pltpu.SemaphoreType.DMA((n_cb,)),
            pltpu.SemaphoreType.DMA,
            pltpu.SemaphoreType.DMA,
            pltpu.SemaphoreType.DMA((13,)),
            pltpu.SemaphoreType.DMA((units,)),
            pltpu.SemaphoreType.DMA((4,)),
            pltpu.SemaphoreType.DMA((2, units)),
            pltpu.SemaphoreType.DMA((2, units)),
            pltpu.SemaphoreType.DMA((2,)),
        ],
        compiler_params=pltpu.CompilerParams(
            collective_id=0, has_side_effects=True, vmem_limit_bytes=60 * 2**20
        ),
        name="exchange",
    )(m_slot[None, :], comp, grid, mix)


def expand_kernel(m_slot, q_hbm, s_hbm, e_ref, out_hbm, q_ref, s_ref, held, q_sem, s_sem, out_sem):
    slots, _, degrees = e_ref.shape
    chunks = slots // UNIT
    cols = WIDE * CB

    def load(k):
        part = pl.ds(k * chunks, chunks)
        return pltpu.make_async_copy(q_hbm.at[part], q_ref.at[part], q_sem.at[k])

    scales = pltpu.make_async_copy(s_hbm, s_ref, s_sem)
    for k in range(WIDE):
        load(k).start()
    scales.start()
    for k in range(WIDE, q_ref.shape[0] // chunks):
        load(k).start()
    my_z = lax.rem(lax.axis_index("fly"), GROUP)
    first = lax.axis_index("fly") * degrees
    base = lax.axis_index("wave") * slots
    degree = first + lax.broadcasted_iota(I32, (degrees, cols), 0)
    dot = functools.partial(
        lax.dot_general,
        dimension_numbers=(((0,), (0,)), ((), ())),
        preferred_element_type=F32,
    )
    scales.wait()

    def piece(p, _):
        block, ch = p // chunks, lax.rem(p, chunks)

        @pl.when(ch == 0)
        def _():
            for k in range(WIDE):
                load(block * WIDE + k).wait()

        us = [(block * WIDE + k) * chunks + ch for k in range(WIDE)]
        vals = []
        for i in range(UNIT):
            half, j = i // GROUP, i % GROUP
            x = lax.rem(j + my_z + 2 * half, GROUP)
            eh, el = split(e_ref[ch * UNIT + i])
            q = jnp.concatenate([q_ref[u, x, half].astype(I32).astype(F32) for u in us], axis=1)
            qh, ql = split(q)
            left, right = jnp.concatenate([eh, eh, el], axis=0), jnp.concatenate([qh, ql, qh], axis=0)
            val = dot(left, right) * jnp.concatenate([s_ref[u, x, half] for u in us], axis=1)
            vals.append(jnp.where(degree >= m_slot[base + ch * UNIT + i], val, 0.0))
        for c in range(0, cols, 128):
            part = jnp.stack([v[:, c : c + 128] for v in vals])
            held[p, :, :, c : c + 128] = pltpu.einshape("sdc->dsc", part)
        to = out_hbm.at[
            :,
            pl.ds(pl.multiple_of(ch * UNIT, UNIT), UNIT),
            pl.ds(pl.multiple_of(block * cols, cols), cols),
        ]
        pltpu.make_async_copy(held.at[p], to, out_sem).start()
        return 0

    lax.fori_loop(0, held.shape[0], piece, 0)
    pltpu.make_async_copy(held, held, out_sem).wait()


def expand_out(m_slot, q, s, exp_t):
    units = q.shape[0]
    slots, _, degrees = exp_t.shape
    n_cb = units * UNIT // slots
    return pl.pallas_call(
        expand_kernel,
        out_shape=jax.ShapeDtypeStruct((degrees, slots, n_cb * CB), F32),
        in_specs=[
            pl.BlockSpec(memory_space=pltpu.SMEM),
            pl.BlockSpec(memory_space=pl.ANY),
            pl.BlockSpec(memory_space=pl.ANY),
            pl.BlockSpec(memory_space=pltpu.VMEM),
        ],
        out_specs=pl.BlockSpec(memory_space=pl.ANY),
        scratch_shapes=[
            pltpu.VMEM(q.shape, I16),
            pltpu.VMEM(s.shape, F32),
            pltpu.VMEM((units // WIDE, degrees, UNIT, WIDE * CB), F32),
            pltpu.SemaphoreType.DMA((n_cb,)),
            pltpu.SemaphoreType.DMA,
            pltpu.SemaphoreType.DMA,
        ],
        compiler_params=pltpu.CompilerParams(vmem_limit_bytes=60 * 2**20),
        name="expand_out",
    )(m_slot, q, s, exp_t)


def on_device(grid_fourier, m_slot, compress, mix, expand):
    comp = jnp.transpose(compress, (1, 2, 0))
    exp_t = jnp.transpose(expand, (1, 2, 0))
    waves = lax.axis_size("wave")
    q, s = exchange(m_slot, comp, grid_fourier, mix[0], waves)
    return expand_out(m_slot, q, s, exp_t)


def solution(mesh):
    in_specs = (
        P(("fly", "wave"), None, None),
        P(),
        P("fly", "wave", None),
        P("fly", "wave", None, None),
        P("fly", "wave", None),
    )
    return jax.shard_map(
        on_device, mesh=mesh, in_specs=in_specs, out_specs=P("fly", "wave", None),
        check_vma=False,
    )
```

```python
import functools

import jax
import jax.numpy as jnp
from jax import lax
from jax.experimental import pallas as pl
from jax.experimental.pallas import tpu as pltpu
from jax.sharding import PartitionSpec as P

MESH = pl.DeviceIdType.MESH
F32, BF16, I16, I32 = jnp.float32, jnp.bfloat16, jnp.int16, jnp.int32

CB = 128
GROUP = 4
HALVES = 2
UNIT = GROUP * HALVES
WIDE = 3
LAG = 3
LEAD = 4
QMAX = 32766.0


def quantize(x):
    largest = jnp.maximum(jnp.max(jnp.abs(x), axis=0, keepdims=True), 1e-30)
    q = jnp.round(x * (QMAX / largest)).astype(I32).astype(I16)
    return q, largest * (1.0 / QMAX)


def restore(q, scale):
    return q.astype(I32).astype(F32) * scale


def split(x):
    high = x.astype(BF16)
    return high, (x - high.astype(F32)).astype(BF16)


def product(ah, al, b):
    bh, bl = split(b)
    left = jnp.concatenate([ah, ah, al], axis=1)
    return jnp.dot(left, jnp.concatenate([bh, bl, bh], axis=0), preferred_element_type=F32)


def pairs(level):
    return [(b, b | 1 << level) for b in range(GROUP) if not b >> level & 1]


def exchange_kernel(
    m_slot, comp_hbm, grid, mix, out_q, out_s,
    gbuf, flat, ysend, yrecv, mixf,
    mzs, mzss, mzr, mzrs, mxs, mxss, mxr, mxrs, fzh, fzl, fxh, fxl,
    z1s, z1ss, z1r, z1rs, z2s, z2ss, x1r, x1rs, x2s, x2ss,
    onehot, comp, load_sem, comp_sem, mix_sem, send_sem, y_sem, m_sem, z1_sem, x1_sem, o_sem,
):
    units, lats = ysend.shape[0], ysend.shape[2]
    waves = ysend.shape[1] // UNIT
    n_cb = gbuf.shape[0]
    chunks = units // n_cb
    w, f = lax.axis_index("wave"), lax.axis_index("fly")
    my_x, my_z = f // GROUP, lax.rem(f, GROUP)

    def z_dev(j):
        return (w, my_x * GROUP + j)

    def x_dev(j):
        return (w, j * GROUP + my_z)

    def other(mine, d):
        return lax.rem(mine + d, GROUP)

    for cb in range(n_cb):
        pltpu.make_async_copy(
            grid.at[:, :, pl.ds(cb * CB, CB)], gbuf.at[cb], load_sem.at[cb]
        ).start()
    pltpu.make_async_copy(comp_hbm, comp, comp_sem).start()
    pltpu.make_async_copy(mix, mixf, mix_sem).start()

    barrier = pltpu.get_barrier_semaphore()
    peers = [(lax.rem(w + d, waves), f) for d in range(1, waves)]
    peers += [(w, lax.rem(f + d, GROUP * GROUP)) for d in range(1, GROUP * GROUP)]
    for peer in peers:
        pl.semaphore_signal(barrier, inc=1, device_id=peer, device_id_type=MESH)

    sent = pl.ds(0, GROUP - 1)

    def push(src, dst, send, recv, peer):
        pltpu.make_async_remote_copy(
            src_ref=src, dst_ref=dst, send_sem=send, recv_sem=recv,
            device_id=peer, device_id_type=MESH,
        ).start()

    def arrive(ref, sem):
        pltpu.make_async_copy(ref, ref, sem).wait()

    def pick(cb, l):
        flat[lax.rem(cb, 2), l] = jnp.dot(onehot[...], gbuf[cb, l], preferred_element_type=F32)

    def arrange(u):
        cb, ch = u // chunks, lax.rem(u, chunks)
        for r in range(0, waves * UNIT, 8):
            rows = pl.ds(pl.multiple_of(ch * (waves * UNIT) + r, 8), 8)
            for c in range(0, CB, 128):
                x = flat[lax.rem(cb, 2), :, rows, c : c + 128]
                ysend[u, r : r + 8, :, c : c + 128] = pltpu.einshape("lsc->slc", x).astype(BF16)

    def send_wave(u):
        dst = yrecv.at[u, :, pl.ds(pl.multiple_of(w * lats, lats), lats), :]
        for d in range(1, waves):
            to = lax.rem(w + d, waves)
            push(ysend.at[u, pl.ds(to * UNIT, UNIT)], dst, send_sem.at[0], y_sem.at[u], (to, f))
        pltpu.make_async_copy(ysend.at[u, pl.ds(w * UNIT, UNIT)], dst, y_sem.at[u]).start()

    def stage_gather(u):
        arrange(u)
        send_wave(u)
        pick_next(u)

    def pick_next(u):
        cb, ch = u // chunks, lax.rem(u, chunks)
        for k in range(1, n_cb):
            first = (k - 1) * chunks
            pl.when(u == first)(lambda k=k: arrive(gbuf.at[k], load_sem.at[k]))

        @pl.when(cb + 1 < n_cb)
        def _():
            for i in range(lats // chunks):
                pick(cb + 1, ch * (lats // chunks) + i)

    def high_dev(j, b, half):
        return lax.rem(j + b + 2 * half, GROUP)

    def prepare_mix():
        arrive(mixf, mix_sem)

        def one(ch, _):
            for j in range(GROUP):
                for level in range(4):
                    q, s = quantize(mixf[ch * GROUP + j, level * 64 : (level + 1) * 64, :])
                    if level < 2:
                        sq, ss, to = mzs, mzss, j
                    else:
                        sq, ss, to = mxs, mxss, high_dev(j, my_z, lax.rem(ch, HALVES))
                    sq[to, ch, (level % 2) * 64 : (level % 2 + 1) * 64, :] = q
                    ss[to, ch, level % 2] = s
            return 0

        lax.fori_loop(0, chunks * HALVES, one, 0)

    def send_mix():
        for mine, dev, sq, ss, rq, rs, k in (
            (my_z, z_dev, mzs, mzss, mzr, mzrs, 0),
            (my_x, x_dev, mxs, mxss, mxr, mxrs, 1),
        ):
            for d in range(1, GROUP):
                j = other(mine, d)
                push(sq.at[j], rq.at[mine], send_sem.at[1 + k], m_sem.at[2 * k], dev(j))
                push(ss.at[j], rs.at[mine], send_sem.at[3 + k], m_sem.at[2 * k + 1], dev(j))
            pltpu.make_async_copy(sq.at[mine], rq.at[mine], m_sem.at[2 * k]).start()
            pltpu.make_async_copy(ss.at[mine], rs.at[mine], m_sem.at[2 * k + 1]).start()

    def copy_pair(sq, ss, dq, ds, k, qsem, ssem, peer):
        if peer is None:
            pltpu.make_async_copy(sq, dq, qsem).start()
            pltpu.make_async_copy(ss, ds, ssem).start()
        else:
            push(sq, dq, send_sem.at[k], qsem, peer)
            push(ss, ds, send_sem.at[k + 1], ssem, peer)

    def stage_compress(u):
        ch = lax.rem(u, chunks)
        pl.when(u == 0)(lambda: arrive(comp, comp_sem))
        arrive(yrecv.at[u], y_sem.at[u])
        for d in (2, 1, 3, 0):
            j = other(my_z, d)
            for half in range(HALVES):
                i = half * GROUP + j
                acc = jnp.dot(comp[ch * UNIT + i], yrecv[u, i], preferred_element_type=F32)
                if d:
                    z1s[u, j, half], z1ss[u, j, half] = quantize(acc)
                else:
                    z1r[u, my_z, half], z1rs[u, my_z, half] = quantize(acc)
            if d:
                copy_pair(
                    z1s.at[u, j], z1ss.at[u, j], z1r.at[u, my_z], z1rs.at[u, my_z],
                    5, z1_sem.at[0, u], z1_sem.at[1, u], z_dev(j),
                )

    def factors(c, mq, ms, fh, fl):
        for level in range(2):
            for pair, (lower, upper) in enumerate(pairs(level)):
                for half, b in enumerate((lower, upper)):
                    x = restore(mq[b, c, level * 64 : (level + 1) * 64, :], ms[b, c, level])
                    rows = slice(half * 64, (half + 1) * 64)
                    fh[c, level, pair, rows], fl[c, level, pair, rows] = split(x)

    def two_levels(u, ch, rq, rs, fh, fl, sq, ss):
        for half in range(HALVES):
            c = ch * HALVES + half
            blocks = [restore(rq[u, b, half], rs[u, b, half]) for b in range(GROUP)]
            for level in range(2):
                new = list(blocks)
                for pair, (lower, upper) in enumerate(pairs(level)):
                    both = jnp.concatenate([blocks[lower], blocks[upper]], axis=0)
                    out = product(fh[c, level, pair], fl[c, level, pair], both)
                    new[lower], new[upper] = out[:64], out[64:]
                blocks = new
            for b in range(GROUP):
                sq[u, b, half], ss[u, b, half] = quantize(blocks[b])

    def stage_low(u):
        ch = lax.rem(u, chunks)

        @pl.when(u == 0)
        def _():
            arrive(mzr, m_sem.at[0])
            arrive(mzrs, m_sem.at[1])

        @pl.when(u < chunks)
        def _():
            for half in range(HALVES):
                factors(ch * HALVES + half, mzr, mzrs, fzh, fzl)


        arrive(z1r.at[u, sent], z1_sem.at[0, u])
        arrive(z1rs.at[u, sent], z1_sem.at[1, u])
        two_levels(u, ch, z1r, z1rs, fzh, fzl, z2s, z2ss)
        for d in (2, 1, 3, 0):
            b = other(my_z, d)
            for half in range(HALVES):
                to = high_dev(my_z, b, half)

                def go(peer, b=b, half=half, k=7 if d else 11):
                    copy_pair(
                        z2s.at[u, b, half], z2ss.at[u, b, half],
                        x1r.at[u, my_x, half], x1rs.at[u, my_x, half],
                        k, x1_sem.at[0, u], x1_sem.at[1, u], peer,
                    )

                if d:
                    go((w, to * GROUP + b))
                else:
                    pl.when(to == my_x)(functools.partial(go, None))
                    pl.when(to != my_x)(functools.partial(go, (w, to * GROUP + b)))

    def stage_high(u):
        ch = lax.rem(u, chunks)

        @pl.when(u == 0)
        def _():
            arrive(mxr, m_sem.at[2])
            arrive(mxrs, m_sem.at[3])

        @pl.when(u < chunks)
        def _():
            for half in range(HALVES):
                factors(ch * HALVES + half, mxr, mxrs, fxh, fxl)


        arrive(x1r.at[u], x1_sem.at[0, u])
        arrive(x1rs.at[u], x1_sem.at[1, u])
        two_levels(u, ch, x1r, x1rs, fxh, fxl, x2s, x2ss)
        for d in (2, 1, 3, 0):
            j = other(my_x, d)
            copy_pair(
                x2s.at[u, j], x2ss.at[u, j], out_q.at[u, my_x], out_s.at[u, my_x],
                9, o_sem.at[0], o_sem.at[1], x_dev(j) if d else None,
            )

    shape = onehot.shape
    row, col = (lax.broadcasted_iota(I32, shape, d) for d in range(2))
    per_chunk = waves * UNIT
    slot = (row % per_chunk // UNIT) * (chunks * UNIT) + row // per_chunk * UNIT + row % UNIT
    onehot[...] = lax.dot_general(
        (col == slot).astype(BF16), (row == m_slot[...]).astype(BF16),
        (((1,), (1,)), ((), ())), preferred_element_type=F32,
    ).astype(BF16)
    arrive(gbuf.at[0], load_sem.at[0])

    def pick_first(l, _):
        pick(0, l)
        return 0

    lax.fori_loop(0, lats, pick_first, 0)
    arrange(0)
    prepare_mix()
    pl.semaphore_wait(barrier, len(peers))
    send_wave(0)
    send_mix()
    pick_next(0)

    def step(t, _):
        for lag, stage in (
            (LEAD + 2 * LAG, stage_high),
            (LEAD + LAG, stage_low),
            (LEAD, stage_compress),
            (0, stage_gather),
        ):
            u = t - lag
            pl.when((u >= 0) & (u < units))(functools.partial(stage, u))
        return 0

    lax.fori_loop(1, units + LEAD + 2 * LAG, step, 0)

    arrive(out_q, o_sem.at[0])
    arrive(out_s, o_sem.at[1])
    arrive(ysend.at[:, pl.ds(0, (waves - 1) * UNIT)], send_sem.at[0])
    for k, ref in enumerate((mzs, mxs, mzss, mxss)):
        arrive(ref.at[sent], send_sem.at[1 + k])
    for k, ref in enumerate((z1s, z1ss)):
        arrive(ref.at[:, sent], send_sem.at[5 + k])
    for k, ref in enumerate((z2s, z2ss)):
        arrive(ref.at[:, sent], send_sem.at[7 + k])
    for k, ref in enumerate((x2s, x2ss)):
        arrive(ref.at[:, sent], send_sem.at[9 + k])
    far = lax.rem(my_x, 2) == 1
    for k, ref in enumerate((z2s, z2ss)):
        pl.when(far)(lambda k=k, ref=ref: arrive(ref.at[:, 0], send_sem.at[11 + k]))
        half = ref.at[:, 0, 0]
        pl.when(jnp.logical_not(far))(lambda k=k, half=half: arrive(half, send_sem.at[11 + k]))


def exchange(m_slot, comp, grid, mix, waves):
    lats, all_slots, cols = grid.shape
    slots, rank, width = comp.shape
    n_cb = cols // CB
    chunks = slots // UNIT
    units = n_cb * chunks
    parts = (units, GROUP, HALVES, rank, CB)
    scales = (units, GROUP, HALVES, 1, CB)
    mq = (GROUP, chunks * HALVES, 2 * rank, 2 * rank)
    ms = (GROUP, chunks * HALVES, 2, 1, 2 * rank)
    vmem = pltpu.VMEM
    any_spec = pl.BlockSpec(memory_space=pl.ANY)
    return pl.pallas_call(
        exchange_kernel,
        out_shape=(jax.ShapeDtypeStruct(parts, I16), jax.ShapeDtypeStruct(scales, F32)),
        in_specs=[
            pl.BlockSpec(memory_space=pltpu.VMEM),
            any_spec,
            any_spec,
            any_spec,
        ],
        out_specs=(any_spec, any_spec),
        scratch_shapes=[
            vmem((n_cb, lats, all_slots, CB), BF16),
            vmem((2, lats, all_slots, CB), F32),
            vmem((units, waves * UNIT, lats, CB), BF16),
            vmem((units, UNIT, width, CB), BF16),
            vmem(mix.shape, F32),
            vmem(mq, I16), vmem(ms, F32), vmem(mq, I16), vmem(ms, F32),
            vmem(mq, I16), vmem(ms, F32), vmem(mq, I16), vmem(ms, F32),
            *[vmem((chunks * HALVES, 2, 2, 2 * rank, 2 * rank), BF16)] * 4,
            vmem(parts, I16), vmem(scales, F32), vmem(parts, I16), vmem(scales, F32),
            vmem(parts, I16), vmem(scales, F32),
            vmem(parts, I16), vmem(scales, F32),
            vmem(parts, I16), vmem(scales, F32),
            vmem((all_slots, all_slots), BF16),
            vmem(comp.shape, BF16),
            pltpu.SemaphoreType.DMA((n_cb,)),
            pltpu.SemaphoreType.DMA,
            pltpu.SemaphoreType.DMA,
            pltpu.SemaphoreType.DMA((13,)),
            pltpu.SemaphoreType.DMA((units,)),
            pltpu.SemaphoreType.DMA((4,)),
            pltpu.SemaphoreType.DMA((2, units)),
            pltpu.SemaphoreType.DMA((2, units)),
            pltpu.SemaphoreType.DMA((2,)),
        ],
        compiler_params=pltpu.CompilerParams(
            collective_id=0, has_side_effects=True, vmem_limit_bytes=60 * 2**20
        ),
        name="exchange",
    )(m_slot[None, :], comp, grid, mix)


def expand_kernel(m_slot, q_hbm, s_hbm, e_ref, out_hbm, q_ref, s_ref, held, q_sem, s_sem, out_sem):
    slots, _, degrees = e_ref.shape
    chunks = slots // UNIT
    cols = WIDE * CB

    def load(k):
        part = pl.ds(k * chunks, chunks)
        return pltpu.make_async_copy(q_hbm.at[part], q_ref.at[part], q_sem.at[k])

    scales = pltpu.make_async_copy(s_hbm, s_ref, s_sem)
    for k in range(WIDE):
        load(k).start()
    scales.start()
    for k in range(WIDE, q_ref.shape[0] // chunks):
        load(k).start()
    my_z = lax.rem(lax.axis_index("fly"), GROUP)
    first = lax.axis_index("fly") * degrees
    base = lax.axis_index("wave") * slots
    degree = first + lax.broadcasted_iota(I32, (degrees, cols), 0)
    dot = functools.partial(
        lax.dot_general,
        dimension_numbers=(((0,), (0,)), ((), ())),
        preferred_element_type=F32,
    )
    scales.wait()

    def piece(p, _):
        block, ch = p // chunks, lax.rem(p, chunks)

        @pl.when(ch == 0)
        def _():
            for k in range(WIDE):
                load(block * WIDE + k).wait()

        us = [(block * WIDE + k) * chunks + ch for k in range(WIDE)]
        vals = []
        for i in range(UNIT):
            half, j = i // GROUP, i % GROUP
            x = lax.rem(j + my_z + 2 * half, GROUP)
            eh, el = split(e_ref[ch * UNIT + i])
            q = jnp.concatenate([q_ref[u, x, half].astype(I32).astype(F32) for u in us], axis=1)
            qh, ql = split(q)
            left, right = jnp.concatenate([eh, eh, el], axis=0), jnp.concatenate([qh, ql, qh], axis=0)
            val = dot(left, right) * jnp.concatenate([s_ref[u, x, half] for u in us], axis=1)
            vals.append(jnp.where(degree >= m_slot[base + ch * UNIT + i], val, 0.0))
        for c in range(0, cols, 128):
            part = jnp.stack([v[:, c : c + 128] for v in vals])
            held[p, :, :, c : c + 128] = pltpu.einshape("sdc->dsc", part)
        to = out_hbm.at[
            :,
            pl.ds(pl.multiple_of(ch * UNIT, UNIT), UNIT),
            pl.ds(pl.multiple_of(block * cols, cols), cols),
        ]
        pltpu.make_async_copy(held.at[p], to, out_sem).start()
        return 0

    lax.fori_loop(0, held.shape[0], piece, 0)
    pltpu.make_async_copy(held, held, out_sem).wait()


def expand_out(m_slot, q, s, exp_t):
    units = q.shape[0]
    slots, _, degrees = exp_t.shape
    n_cb = units * UNIT // slots
    return pl.pallas_call(
        expand_kernel,
        out_shape=jax.ShapeDtypeStruct((degrees, slots, n_cb * CB), F32),
        in_specs=[
            pl.BlockSpec(memory_space=pltpu.SMEM),
            pl.BlockSpec(memory_space=pl.ANY),
            pl.BlockSpec(memory_space=pl.ANY),
            pl.BlockSpec(memory_space=pltpu.VMEM),
        ],
        out_specs=pl.BlockSpec(memory_space=pl.ANY),
        scratch_shapes=[
            pltpu.VMEM(q.shape, I16),
            pltpu.VMEM(s.shape, F32),
            pltpu.VMEM((units // WIDE, degrees, UNIT, WIDE * CB), F32),
            pltpu.SemaphoreType.DMA((n_cb,)),
            pltpu.SemaphoreType.DMA,
            pltpu.SemaphoreType.DMA,
        ],
        compiler_params=pltpu.CompilerParams(vmem_limit_bytes=60 * 2**20),
        name="expand_out",
    )(m_slot, q, s, exp_t)


def on_device(grid_fourier, m_slot, compress, mix, expand):
    comp = jnp.transpose(compress, (1, 2, 0))
    exp_t = jnp.transpose(expand, (1, 2, 0))
    waves = lax.axis_size("wave")
    q, s = exchange(m_slot, comp, grid_fourier, mix[0], waves)
    return expand_out(m_slot, q, s, exp_t)


def solution(mesh):
    in_specs = (
        P(("fly", "wave"), None, None),
        P(),
        P("fly", "wave", None),
        P("fly", "wave", None, None),
        P("fly", "wave", None),
    )
    return jax.shard_map(
        on_device, mesh=mesh, in_specs=in_specs, out_specs=P("fly", "wave", None),
        check_vma=False,
    )
```
